512 devices in a mesh: section: 32 (over z_hi, y), dp: 16 (over z_lo, x, core).
Axes of the slice: x: 4, y: 8, z: 8 (z_hi: 4, z_lo: 2; z = z_hi * 2 + z_lo), core: 2. Of those that a mesh axis runs over, the one named last changes fastest.
Arguments:
- saved_input: bfloat16 [32, 2048, 12288], P('section', 'dp'), may hold values from -6 to 6
- norm_gain: float32 [32, 12288], P('section'), may hold values from 0.25 to 1.75
- left_in: bfloat16 [32, 2048, 64], P('section', 'dp'), may hold values from -6 to 6
- right_in: bfloat16 [32, 12288, 64], P('section', 'dp'), may hold values from -0.75 to 0.75
- basis: bfloat16 [32, 12288, 64], P('section', 'dp'), may hold values from -0.0546875 to 0.0546875
Outputs:
- gain_grad: float32 [32, 12288], P('section', 'dp')
- bias_grad: float32 [32, 12288], P('section', 'dp')
- left_out: bfloat16 [32, 2048, 64], P('section', 'dp')
- right_out: bfloat16 [32, 12288, 64], P('section', 'dp')
The draws below stay inside these ranges and needn't reach their ends.
All inputs are finite; a program needn't handle non-finite values.
Results may differ from the reference program's by a relative error of at most 0.02.
Values may be sent and summed in bfloat16 or wider, within the bound.
No kernel may reach another device: no remote copies, remote signals or barrier semaphores. Data moves between devices by JAX's collectives and lax.ppermute only.
A program may use at most 64 MiB of HBM per device.

```python
import jax
import jax.numpy as jnp
from jax import lax

D = 12288
R = 64
TOKENS = 2048
SECTIONS = 32


def shard_levels(own_key, dims, shards, least, top_value):
    def one(position, shards_of):
        steps = jax.random.uniform(jax.random.fold_in(jax.random.fold_in(own_key, 6), position), (shards_of,), jnp.float32, least / len(shards), top_value / len(shards))
        return jnp.repeat(jnp.exp(steps), dims[position] // shards_of).reshape((-1,) + (1,) * (len(dims) - position - 1))

    level = one(*shards[0])
    for cut in shards[1:]:
        level = level * one(*cut)
    return level


def normal_values(own_key, extent, width, bound, cuts=(), kind=jnp.bfloat16):
    array = width * jax.random.normal(own_key, extent, jnp.float32)
    if cuts:
        array = array * shard_levels(own_key, extent, cuts, -0.22, 0.18)
    return jnp.clip(array, -bound, bound).astype(kind)


def setup_inputs(seed: int = 0) -> dict:
    arg_keys = jax.random.split(jax.random.key(seed), 6)
    saved_input = normal_values(arg_keys[0], (SECTIONS, TOKENS, D), 1.0, 6.0, ((0, 32), (1, 16)))
    norm_gain = jnp.clip(1.0 + 0.15 * jax.random.normal(arg_keys[1], (SECTIONS, D), jnp.float32), 0.25, 1.75)
    left_in = normal_values(arg_keys[2], (SECTIONS, TOKENS, R), 1.0, 6.0, ((0, 32), (1, 16)))
    right_in = normal_values(arg_keys[3], (SECTIONS, D, R), R ** -0.5, 0.75, ((0, 32), (1, 16)))
    basis = normal_values(arg_keys[4], (SECTIONS, D, R), D ** -0.5, 0.0546875, ((0, 32), (1, 16)))
    return dict(saved_input=saved_input, norm_gain=norm_gain, left_in=left_in, right_in=right_in, basis=basis)


def section_step(items):
    saved, gain, left, right, basis = items
    rebuilt = jnp.dot(left.astype(jnp.float32), right.T.astype(jnp.float32), preferred_element_type=jnp.float32)
    values = saved.astype(jnp.float32)
    center = values - lax.optimization_barrier(jnp.mean(values, axis=1, keepdims=True))
    inverse = lax.rsqrt(lax.optimization_barrier(jnp.mean(center * center, axis=1, keepdims=True)) + 1e-05)
    normed = center * inverse
    factor = 1.0 / jnp.sqrt(jnp.float32(TOKENS))
    gain_term = lax.optimization_barrier(jnp.sum(rebuilt * normed, axis=0)) * factor
    bias_term = lax.optimization_barrier(jnp.sum(rebuilt, axis=0)) * factor
    scaled = rebuilt * gain[None, :]
    first = lax.optimization_barrier(jnp.mean(scaled, axis=1, keepdims=True))
    second = lax.optimization_barrier(jnp.mean(scaled * normed, axis=1, keepdims=True))
    boundary = (inverse * (scaled - first - normed * second)).astype(jnp.bfloat16)
    power = jnp.dot(boundary.astype(jnp.float32), basis.astype(jnp.float32), preferred_element_type=jnp.float32)
    gram = jnp.dot(power.T, power, precision=lax.Precision.HIGHEST)
    lower = jnp.linalg.cholesky(gram)
    ortho = jax.scipy.linalg.solve_triangular(lower, power.T, lower=True).T.astype(jnp.bfloat16)
    feature = jnp.dot(boundary.T.astype(jnp.float32), ortho.astype(jnp.float32), preferred_element_type=jnp.float32).astype(jnp.bfloat16)
    return (ortho, feature, gain_term, bias_term)

def reference(saved_input, norm_gain, left_in, right_in, basis):
    ortho, feature, gain_grad, bias_grad = lax.map(section_step, (saved_input, norm_gain, left_in, right_in, basis))
    left_out = jnp.concatenate([ortho[1:], jnp.zeros_like(ortho[:1])], axis=0)
    right_out = jnp.concatenate([feature[1:], jnp.zeros_like(feature[:1])], axis=0)
    return (gain_grad, bias_grad, left_out, right_out)
```

```python
import jax
import jax.numpy as jnp
from jax import lax
from jax.experimental import pallas as pl
from jax.experimental.pallas import tpu as pltpu
from jax.sharding import PartitionSpec as P

LANES = 128
F32 = jnp.float32
BF16 = jnp.bfloat16
NT = (((1,), (1,)), ((), ()))


def main_kernel(parity, x, gain, left_t, full, keep, send, power_t, rebuilt, boundary, rows, tail):
    blocks, _, width = full.shape
    tokens = x.shape[0]
    features = blocks * width
    rank = power_t.shape[0]
    chunks = width // LANES
    zero = jnp.zeros((tokens, LANES), F32)

    def columns(j, c):
        return pl.ds(pl.multiple_of(j * width + c * LANES, LANES), LANES)

    def row_mean(total):
        return jnp.broadcast_to(jnp.sum(total, axis=1, keepdims=True) * (1.0 / features), total.shape)

    def add(j, total):
        for c in range(chunks):
            total = total + x[:, columns(j, c)].astype(F32)
        return total

    rows[0] = row_mean(lax.fori_loop(0, blocks, add, zero))

    def add_squares(j, total):
        for c in range(chunks):
            center = x[:, columns(j, c)].astype(F32) - rows[0]
            total = total + center * center
        return total

    rows[1] = lax.rsqrt(row_mean(lax.fori_loop(0, blocks, add_squares, zero)) + 1e-05)

    left = left_t[...].astype(F32).T.astype(BF16)

    rows[2] = zero
    rows[3] = zero
    for side, out in enumerate((keep, send)):
        own = parity[0] ^ side

        @pl.loop(0, blocks // 2)
        def _(k):
            j = 2 * k + own
            rebuilt[j] = jnp.dot(left, full[j, :rank, :], preferred_element_type=F32)
            first, second = rows[2], rows[3]
            for c in range(chunks):
                lanes = slice(c * LANES, (c + 1) * LANES)
                part = rebuilt[j, :, lanes]
                normed = (x[:, columns(j, c)].astype(F32) - rows[0]) * rows[1]
                scaled = part * gain[:, columns(j, c)]
                first = first + scaled
                second = second + scaled * normed
                out[k, rank : rank + 1, lanes] = jnp.sum(part * normed, axis=0, keepdims=True)
                out[k, rank + 1 : rank + 2, lanes] = jnp.sum(part, axis=0, keepdims=True)
            rows[2] = first
            rows[3] = second

    rows[2] = row_mean(rows[2])
    rows[3] = row_mean(rows[3])

    def project(j, total):
        for c in range(chunks):
            lanes = slice(c * LANES, (c + 1) * LANES)
            normed = (x[:, columns(j, c)].astype(F32) - rows[0]) * rows[1]
            scaled = rebuilt[j, :, lanes] * gain[:, columns(j, c)]
            boundary[j, :, lanes] = (rows[1] * (scaled - rows[2] - normed * rows[3])).astype(BF16)
        return total + lax.dot_general(full[j, rank:, :], boundary[j], NT, preferred_element_type=F32)

    power = lax.fori_loop(0, blocks, project, jnp.zeros((rank, tokens), F32))
    power_t[...] = power
    gram = lax.dot_general(power, power, NT, precision=lax.Precision.HIGHEST, preferred_element_type=F32)
    half = rank // 2
    tail[...] = jnp.zeros_like(tail)
    packed = jnp.concatenate([gram[:half], gram[half:]], axis=1)
    for q in range(half):
        tail[q // chunks : q // chunks + 1, (q % chunks) * LANES : (q % chunks + 1) * LANES] = packed[q : q + 1]
    high = power.astype(BF16)
    low = (power - high.astype(F32)).astype(BF16)
    both = jnp.concatenate([high, low], axis=0)

    for side, out in enumerate((keep, send)):
        own = parity[0] ^ side

        @pl.loop(0, blocks // 2)
        def _(k):
            terms = jnp.dot(both, boundary[2 * k + own], preferred_element_type=F32)
            out[k, :rank, :] = terms[:rank] + terms[rank:]
            out[k, rank + 2 :, :] = tail[: out.shape[1] - rank - 2]


def inverse_factor(gram):
    size = gram.shape[0]
    wide = 2 * size
    row = lax.broadcasted_iota(jnp.int32, (size, size), 0)
    col = lax.broadcasted_iota(jnp.int32, (size, size), 1)
    eye = jnp.where(row == col, 1.0, 0.0).astype(F32)
    work = jnp.concatenate([gram, eye], axis=1)
    parts = [work[8 * i : 8 * i + 8] for i in range(size // 8)]
    below = lax.broadcasted_iota(jnp.int32, (8, wide), 0)
    for k in range(size):
        at, r = divmod(k, 8)
        pivot = jnp.broadcast_to(parts[at][r : r + 1], (8, wide))
        scale = 1.0 / jnp.broadcast_to(pivot[:, k : k + 1], (8, wide))
        pivot = pivot * scale
        for i in range(at, size // 8):
            step = jnp.broadcast_to(parts[i][:, k : k + 1], (8, wide)) * pivot
            if i == at:
                step = jnp.where(below > r, step, 0.0)
            parts[i] = parts[i] - step
    work = jnp.concatenate(parts, axis=0)
    diagonal = jnp.sum(jnp.where(row == col, work[:, :size], 0.0), axis=1, keepdims=True)
    return work[:, size:] * lax.rsqrt(diagonal)


def post_kernel(factor, terms, power_t, gain_out, bias_out, moved, square):
    rank, tokens = power_t.shape
    width = terms.shape[2]
    chunks = width // LANES
    half = rank // 2
    total = terms[0]
    for j in range(1, terms.shape[0]):
        total = total + terms[j]
    gain_out[...] = total[rank : rank + 1] * factor
    bias_out[...] = total[rank + 1 : rank + 2] * factor
    for q in range(half):
        line = rank + 2 + q // chunks
        start = (q % chunks) * LANES
        square[q : q + 1, :] = total[line : line + 1, start : start + LANES]
    packed = square[...]
    inverse = inverse_factor(jnp.concatenate([packed[:, :rank], packed[:, rank:]], axis=0))
    exact = dict(precision=lax.Precision.HIGHEST, preferred_element_type=F32)
    moved[:, :width] = jnp.dot(inverse, total[:rank], **exact).astype(BF16)
    moved[:, width:] = jnp.dot(inverse, power_t[...], **exact).astype(BF16)


def on_device(saved_input, norm_gain, left_in, right_in, basis):
    _, tokens, features = saved_input.shape
    width, rank = right_in.shape[1:]
    replicas = lax.axis_size("dp")
    pairs = replicas // 2
    chunks = width // LANES
    height = rank + 2 + -(-(rank // 2) // chunks)
    vmem = pl.BlockSpec(memory_space=pltpu.VMEM)
    smem = pl.BlockSpec(memory_space=pltpu.SMEM)

    own = jnp.concatenate([right_in[0].T, basis[0].T], axis=0)
    full = lax.all_gather(own, "dp")
    parity = (lax.axis_index("dp") % 2).astype(jnp.int32).reshape(1)
    block = jax.ShapeDtypeStruct((pairs, height, width), F32)
    keep, send, power_t = pl.pallas_call(
        main_kernel,
        out_shape=(block, block, jax.ShapeDtypeStruct((rank, tokens), F32)),
        in_specs=[smem, vmem, vmem, vmem, vmem],
        out_specs=(vmem, vmem, vmem),
        scratch_shapes=[
            pltpu.VMEM((replicas, tokens, width), F32),
            pltpu.VMEM((replicas, tokens, width), BF16),
            pltpu.VMEM((4, tokens, LANES), F32),
            pltpu.VMEM((8, width), F32),
        ],
        compiler_params=pltpu.CompilerParams(vmem_limit_bytes=40 * 2**20),
    )(parity, saved_input[0], norm_gain, left_in[0].T, full)
    other = lax.ppermute(send, "dp", [(i, i ^ 1) for i in range(replicas)])
    groups = [[2 * k + c for k in range(pairs)] for c in range(2)]
    terms = lax.all_to_all(keep + other, "dp", 0, 0, tiled=True, axis_index_groups=groups)

    factor = float(1.0 / (tokens * replicas) ** 0.5)
    gain_grad, bias_grad, moved = pl.pallas_call(
        lambda *refs: post_kernel(factor, *refs),
        out_shape=(
            jax.ShapeDtypeStruct((1, width), F32),
            jax.ShapeDtypeStruct((1, width), F32),
            jax.ShapeDtypeStruct((rank, width + tokens), BF16),
        ),
        in_specs=[vmem, vmem],
        out_specs=(vmem, vmem, vmem),
        scratch_shapes=[pltpu.VMEM((rank // 2, LANES), F32)],
        compiler_params=pltpu.CompilerParams(vmem_limit_bytes=16 * 2**20),
    )(terms, power_t)
    sections = lax.axis_size("section")
    moved = lax.ppermute(moved, "section", [(i, i - 1) for i in range(1, sections)])
    return gain_grad, bias_grad, moved[:, width:].T[None], moved[:, :width].T[None]


def solution(mesh):
    placed = (
        P("section", "dp", None),
        P("section", None),
        P("section", "dp", None),
        P("section", "dp", None),
        P("section", "dp", None),
    )
    return jax.shard_map(
        on_device,
        mesh=mesh,
        in_specs=placed,
        out_specs=(
            P("section", "dp"),
            P("section", "dp"),
            P("section", "dp", None),
            P("section", "dp", None),
        ),
        check_vma=False,
    )
```

```python
import jax
import jax.numpy as jnp
from jax import lax
from jax.experimental import pallas as pl
from jax.experimental.pallas import tpu as pltpu
from jax.sharding import PartitionSpec as P

LANES = 128
GROUP = 16
F32 = jnp.float32
BF16 = jnp.bfloat16
NT = (((1,), (1,)), ((), ()))
VMEM = pl.BlockSpec(memory_space=pltpu.VMEM)
SMEM = pl.BlockSpec(memory_space=pltpu.SMEM)


def fold(value):
    return value[:8] + value[8:]


def gain_pass(j, k, left, factors, x, gain, rows, rebuilt, sums):
    tokens, width = rebuilt.shape[1:]
    rank = left.shape[1]
    rebuilt[k] = jnp.dot(left, factors[k, :rank, :], preferred_element_type=F32)
    chunks = range(width // LANES)
    columns = [pl.ds(pl.multiple_of(j * width + c * LANES, LANES), LANES) for c in chunks]
    gains = [jnp.broadcast_to(gain[:, columns[c]], (GROUP, LANES)) for c in chunks]
    products = [jnp.zeros((8, LANES), F32) for _ in chunks]
    plain = [jnp.zeros((8, LANES), F32) for _ in chunks]
    for r in range(0, tokens, GROUP):
        group = slice(r, r + GROUP)
        mean, inverse = rows[0, group], rows[1, group]
        first, second = rows[2, group], rows[3, group]
        for c in chunks:
            part = rebuilt[k, group, c * LANES : (c + 1) * LANES]
            normed = (x[group, columns[c]].astype(F32) - mean) * inverse
            scaled = part * gains[c]
            first = first + scaled
            second = second + scaled * normed
            products[c] = products[c] + fold(part * normed)
            plain[c] = plain[c] + fold(part)
        rows[2, group] = first
        rows[3, group] = second
    for c in chunks:
        lanes = slice(c * LANES, (c + 1) * LANES)
        sums[k, 0:1, lanes] = jnp.sum(products[c], axis=0, keepdims=True)
        sums[k, 1:2, lanes] = jnp.sum(plain[c], axis=0, keepdims=True)


def row_mean(total, features):
    return jnp.broadcast_to(jnp.sum(total, axis=1, keepdims=True) * (1.0 / features), total.shape)


def first_kernel(parity, x_hbm, gain, left_t, mine, x, left_out, rows, rebuilt, sums, arrived):
    half, _, width = mine.shape
    tokens, features = x.shape
    blocks = 2 * half
    chunks = range(width // LANES)

    def fetch(j):
        columns = pl.ds(pl.multiple_of(j * width, LANES), width)
        return pltpu.make_async_copy(x_hbm.at[:, columns], x.at[:, columns], arrived.at[j])

    @pl.loop(0, blocks)
    def _(j):
        fetch(j).start()

    left_out[...] = left_t[...].astype(F32).T.astype(BF16)
    left = left_out[...]
    rows[...] = jnp.zeros_like(rows)

    @pl.loop(0, blocks)
    def _(j):
        fetch(j).wait()
        for r in range(0, tokens, GROUP):
            group = slice(r, r + GROUP)
            total = rows[0, group]
            for c in chunks:
                columns = pl.ds(pl.multiple_of(j * width + c * LANES, LANES), LANES)
                total = total + x[group, columns].astype(F32)
            rows[0, group] = total

    rows[0] = row_mean(rows[0], features)

    @pl.loop(0, blocks)
    def _(j):
        for r in range(0, tokens, GROUP):
            group = slice(r, r + GROUP)
            total, mean = rows[1, group], rows[0, group]
            for c in chunks:
                columns = pl.ds(pl.multiple_of(j * width + c * LANES, LANES), LANES)
                center = x[group, columns].astype(F32) - mean
                total = total + center * center
            rows[1, group] = total

    rows[1] = lax.rsqrt(row_mean(rows[1], features) + 1e-05)

    @pl.loop(0, half)
    def _(k):
        gain_pass(2 * k + parity[0], k, left, mine, x, gain, rows, rebuilt, sums)


def second_kernel(
    parity, x, gain, left_ref, rows_in, rebuilt_mine, mine, theirs, power_t, both_out, kept, tail, send, rows, rebuilt, sums, moved
):
    half, height, width = theirs.shape
    tokens, features = x.shape
    rank = left_ref.shape[1]
    chunks = range(width // LANES)
    left = left_ref[...]
    rows[...] = rows_in[...]

    @pl.loop(0, half)
    def _(k):
        gain_pass(2 * k + (1 - parity[0]), k, left, theirs, x, gain, rows, rebuilt, sums)

    first = row_mean(rows[2], features)
    second = row_mean(rows[3], features)
    rows[2] = rows[1] * rows[1] * second
    rows[3] = rows[0] * rows[2] - rows[1] * first

    def project(side, factors, source, target):
        def step(k, total):
            j = 2 * k + (parity[0] ^ side)
            columns = [pl.ds(pl.multiple_of(j * width + c * LANES, LANES), LANES) for c in chunks]
            gains = [jnp.broadcast_to(gain[:, columns[c]], (GROUP, LANES)) for c in chunks]
            for r in range(0, tokens, GROUP):
                group = slice(r, r + GROUP)
                inverse, slope, offset = rows[1, group], rows[2, group], rows[3, group]
                for c in chunks:
                    lanes = slice(c * LANES, (c + 1) * LANES)
                    scaled = source[k, group, lanes] * gains[c]
                    value = scaled * inverse - x[group, columns[c]].astype(F32) * slope + offset
                    target[k, group, lanes] = value.astype(BF16)
            return total + lax.dot_general(factors[k, rank:, :], target[k], NT, preferred_element_type=F32)

        return step

    power = lax.fori_loop(0, half, project(0, mine, rebuilt_mine, kept), jnp.zeros((rank, tokens), F32))
    power = lax.fori_loop(0, half, project(1, theirs, rebuilt, moved), power)
    power_t[...] = power
    gram = lax.dot_general(power, power, NT, precision=lax.Precision.HIGHEST, preferred_element_type=F32)
    side = rank // 2
    tail[...] = jnp.zeros_like(tail)
    packed = jnp.concatenate([gram[:side], gram[side:]], axis=1)
    per = width // LANES
    for q in range(side):
        tail[q // per : q // per + 1, (q % per) * LANES : (q % per + 1) * LANES] = packed[q : q + 1]
    high = power.astype(BF16)
    low = (power - high.astype(F32)).astype(BF16)
    both = jnp.concatenate([high, low], axis=0)
    both_out[...] = both
    feature_terms(both, moved, sums, tail, send)


def feature_terms(both, boundary, sums, tail, out):
    half, height, _ = out.shape
    rank = both.shape[0] // 2

    @pl.loop(0, half)
    def _(k):
        terms = jnp.dot(both, boundary[k], preferred_element_type=F32)
        out[k, :rank, :] = terms[:rank] + terms[rank:]
        out[k, rank : rank + 2, :] = sums[k, 0:2, :]
        out[k, rank + 2 :, :] = tail[: height - rank - 2]


def third_kernel(both, kept, sums, tail, keep):
    feature_terms(both[...], kept, sums, tail, keep)


def inverse_factor(gram):
    size = gram.shape[0]
    wide = 2 * size
    count = size // 8
    row = lax.broadcasted_iota(jnp.int32, (size, size), 0)
    col = lax.broadcasted_iota(jnp.int32, (size, size), 1)
    work = jnp.concatenate([gram, jnp.where(row == col, 1.0, 0.0).astype(F32)], axis=1)
    parts = [work[8 * i : 8 * i + 8] for i in range(count)]
    done = []
    for b in range(count):
        lines = [parts[b][r : r + 1] for r in range(8)]
        entry = {
            (i, j): jnp.broadcast_to(lines[i][:, 8 * b + j : 8 * b + j + 1], (1, wide))
            for i in range(8)
            for j in range(i + 1)
        }
        ratio, scale = {}, []
        for r in range(8):
            scale.append(1.0 / entry[r, r])
            for i in range(r + 1, 8):
                ratio[i, r] = entry[i, r] * scale[r]
            for i in range(r + 1, 8):
                for j in range(r + 1, i + 1):
                    entry[i, j] = entry[i, j] - ratio[i, r] * entry[j, r]
                lines[i] = lines[i] - ratio[i, r] * lines[r]
        done += [lines[r] * lax.rsqrt(entry[r, r]) for r in range(8)]
        solved = [None] * 8
        for r in reversed(range(8)):
            solved[r] = lines[r] * scale[r]
            for j in range(r + 1, 8):
                solved[r] = solved[r] - ratio[j, r] * solved[j]
        for i in range(b + 1, count):
            value = parts[i]
            for r in range(8):
                value = value - jnp.broadcast_to(parts[i][:, 8 * b + r : 8 * b + r + 1], (8, wide)) * solved[r]
            parts[i] = value
    return jnp.concatenate(done, axis=0)[:, size:]


def post_kernel(factor, terms, power_t, gain_out, bias_out, moved, square):
    rank, tokens = power_t.shape
    width = terms.shape[2]
    chunks = width // LANES
    half = rank // 2
    total = terms[0]
    for j in range(1, terms.shape[0]):
        total = total + terms[j]
    gain_out[...] = total[rank : rank + 1] * factor
    bias_out[...] = total[rank + 1 : rank + 2] * factor
    for q in range(half):
        line = rank + 2 + q // chunks
        start = (q % chunks) * LANES
        square[q : q + 1, :] = total[line : line + 1, start : start + LANES]
    packed = square[...]
    inverse = inverse_factor(jnp.concatenate([packed[:, :rank], packed[:, rank:]], axis=0))
    exact = dict(precision=lax.Precision.HIGHEST, preferred_element_type=F32)
    moved[:, :width] = jnp.dot(inverse, total[:rank], **exact).astype(BF16)
    moved[:, width:] = jnp.dot(inverse, power_t[...], **exact).astype(BF16)


def limit(mib):
    return pltpu.CompilerParams(vmem_limit_bytes=mib * 2**20)


def cost(mib):
    return pl.CostEstimate(flops=0, bytes_accessed=mib * 2**20, transcendentals=0)


def on_device(saved_input, norm_gain, left_in, right_in, basis):
    _, tokens, features = saved_input.shape
    width, rank = right_in.shape[1:]
    replicas = lax.axis_size("dp")
    half = replicas // 2
    chunks = width // LANES
    height = rank + 2 + -(-(rank // 2) // chunks)
    others = [(i, i ^ 1) for i in range(replicas)]
    groups = [[2 * k + c for k in range(half)] for c in range(2)]
    shape = jax.ShapeDtypeStruct

    own = jnp.concatenate([right_in[0].T, basis[0].T], axis=0)
    copies = jnp.broadcast_to(own[None], (half,) + own.shape)
    mine = lax.all_to_all(copies, "dp", 0, 0, tiled=True, axis_index_groups=groups)
    theirs = lax.ppermute(mine, "dp", others)
    parity = (lax.axis_index("dp") & 1).astype(jnp.int32).reshape(1)
    x, left, rows, rebuilt, sums = pl.pallas_call(
        first_kernel,
        out_shape=(
            shape((tokens, features), BF16),
            shape((tokens, rank), BF16),
            shape((4, tokens, LANES), F32),
            shape((half, tokens, width), F32),
            shape((half, 8, width), F32),
        ),
        in_specs=[SMEM, pl.BlockSpec(memory_space=pltpu.HBM), VMEM, VMEM, VMEM],
        out_specs=(VMEM,) * 5,
        scratch_shapes=[pltpu.SemaphoreType.DMA((replicas,))],
        compiler_params=limit(20),
        cost_estimate=cost(24),
    )(parity, saved_input[0], norm_gain, left_in[0].T, mine)
    power_t, both, kept, tail, send = pl.pallas_call(
        second_kernel,
        out_shape=(
            shape((rank, tokens), F32),
            shape((2 * rank, tokens), BF16),
            shape((half, tokens, width), BF16),
            shape((8, width), F32),
            shape((half, height, width), F32),
        ),
        in_specs=[SMEM] + [VMEM] * 7,
        out_specs=(VMEM,) * 5,
        scratch_shapes=[
            pltpu.VMEM((4, tokens, LANES), F32),
            pltpu.VMEM((half, tokens, width), F32),
            pltpu.VMEM((half, 8, width), F32),
            pltpu.VMEM((half, tokens, width), BF16),
        ],
        compiler_params=limit(32),
    )(parity, x, norm_gain, left, rows, rebuilt, mine, theirs)
    other = lax.ppermute(send, "dp", others)
    keep = pl.pallas_call(
        third_kernel,
        out_shape=shape((half, height, width), F32),
        in_specs=[VMEM] * 4,
        out_specs=VMEM,
        compiler_params=limit(12),
        cost_estimate=cost(12),
    )(both, kept, sums, tail)
    terms = lax.all_to_all(keep + other, "dp", 0, 0, tiled=True, axis_index_groups=groups)

    factor = float(1.0 / (tokens * replicas) ** 0.5)
    gain_grad, bias_grad, moved = pl.pallas_call(
        lambda *refs: post_kernel(factor, *refs),
        out_shape=(shape((1, width), F32), shape((1, width), F32), shape((rank, width + tokens), BF16)),
        in_specs=[VMEM, VMEM],
        out_specs=(VMEM,) * 3,
        scratch_shapes=[pltpu.VMEM((rank // 2, LANES), F32)],
        compiler_params=limit(16),
    )(terms, power_t)
    sections = lax.axis_size("section")
    moved = lax.ppermute(moved, "section", [(i, i - 1) for i in range(1, sections)])
    return gain_grad, bias_grad, moved[:, width:].T[None], moved[:, :width].T[None]


def solution(mesh):
    placed = (
        P("section", "dp", None),
        P("section", None),
        P("section", "dp", None),
        P("section", "dp", None),
        P("section", "dp", None),
    )
    return jax.shard_map(
        on_device,
        mesh=mesh,
        in_specs=placed,
        out_specs=(
            P("section", "dp"),
            P("section", "dp"),
            P("section", "dp", None),
            P("section", "dp", None),
        ),
        check_vma=False,
    )
```

```python
import jax
import jax.numpy as jnp
from jax import lax
from jax.experimental import pallas as pl
from jax.experimental.pallas import tpu as pltpu
from jax.sharding import PartitionSpec as P

LANES = 128
GROUP = 16
UNROLL = 4
F32 = jnp.float32
BF16 = jnp.bfloat16
NT = (((1,), (1,)), ((), ()))
VMEM = pl.BlockSpec(memory_space=pltpu.VMEM)
SMEM = pl.BlockSpec(memory_space=pltpu.SMEM)


def fold(value):
    return value[:8] + value[8:]


def gain_pass(j, k, left, factors, x, gain, rows, rebuilt, sums, plain=True, normal=True):
    tokens, width = rebuilt.shape[1:]
    rank = left.shape[1]
    chunks = range(width // LANES)
    columns = [pl.ds(pl.multiple_of(j * width + c * LANES, LANES), LANES) for c in chunks]
    gains = [jnp.broadcast_to(gain[:, columns[c]], (GROUP, LANES)) for c in chunks]
    products = [jnp.zeros((8, LANES), F32) for _ in chunks]
    bare = [jnp.zeros((8, LANES), F32) for _ in chunks]
    if plain:
        rebuilt[k] = jnp.dot(left, factors[k, :rank, :], preferred_element_type=F32)
    for r in range(0, tokens, GROUP):
        group = slice(r, r + GROUP)
        if normal:
            mean, inverse, second = rows[0, group], rows[1, group], rows[3, group]
        if plain:
            first = rows[2, group]
        for c in chunks:
            part = rebuilt[k, group, c * LANES : (c + 1) * LANES]
            scaled = part * gains[c]
            if plain:
                first = first + scaled
                bare[c] = bare[c] + fold(part)
            if normal:
                normed = (x[group, columns[c]].astype(F32) - mean) * inverse
                second = second + scaled * normed
                products[c] = products[c] + fold(part * normed)
        if plain:
            rows[2, group] = first
        if normal:
            rows[3, group] = second
    for c in chunks:
        lanes = slice(c * LANES, (c + 1) * LANES)
        if normal:
            sums[k, 0:1, lanes] = jnp.sum(products[c], axis=0, keepdims=True)
        if plain:
            sums[k, 1:2, lanes] = jnp.sum(bare[c], axis=0, keepdims=True)


def row_mean(total, features):
    return jnp.broadcast_to(jnp.sum(total, axis=1, keepdims=True) * (1.0 / features), total.shape)


def first_kernel(parity, x_hbm, gain, left_t, mine, x, left_out, rows, rebuilt, sums, arrived):
    half, _, width = mine.shape
    tokens, features = x.shape
    blocks = 2 * half
    chunks = range(width // LANES)

    def fetch(j):
        columns = pl.ds(pl.multiple_of(j * width, LANES), width)
        return pltpu.make_async_copy(x_hbm.at[:, columns], x.at[:, columns], arrived.at[j])

    @pl.loop(0, blocks)
    def _(j):
        fetch(j).start()

    left_out[...] = left_t[...].astype(F32).T.astype(BF16)
    left = left_out[...]
    rows[...] = jnp.zeros_like(rows)

    for j in range(UNROLL):
        fetch(j).wait()
    for r in range(0, tokens, GROUP):
        group = slice(r, r + GROUP)
        total = x[group, :LANES].astype(F32)
        for c in chunks[1:]:
            total = total + x[group, c * LANES : (c + 1) * LANES].astype(F32)
        rows[0, group] = row_mean(total, width)

    @pl.loop(0, blocks // UNROLL)
    def _(step):
        @pl.when(step > 0)
        def _():
            for u in range(UNROLL):
                fetch(step * UNROLL + u).wait()

        for r in range(0, tokens, GROUP):
            group = slice(r, r + GROUP)
            base, total, squares = rows[0, group], rows[1, group], rows[3, group]
            for u in range(UNROLL):
                for c in chunks:
                    start = (step * UNROLL + u) * width + c * LANES
                    center = x[group, pl.ds(pl.multiple_of(start, LANES), LANES)].astype(F32) - base
                    total = total + center
                    squares = squares + center * center
            rows[1, group] = total
            rows[3, group] = squares
        for k in [step * UNROLL // 2 + u for u in range(UNROLL // 2)]:
            gain_pass(2 * k + parity[0], k, left, mine, x, gain, rows, rebuilt, sums, normal=False)

    shift = row_mean(rows[1], features)
    variance = jnp.maximum(row_mean(rows[3], features) - shift * shift, 0.0)
    rows[0] = rows[0] + shift
    rows[1] = lax.rsqrt(variance + 1e-05)
    rows[3] = jnp.zeros((tokens, LANES), F32)

    @pl.loop(0, half // UNROLL)
    def _(step):
        for k in [step * UNROLL + u for u in range(UNROLL)]:
            gain_pass(2 * k + parity[0], k, left, mine, x, gain, rows, rebuilt, sums, plain=False)


def second_kernel(
    parity, x, gain, left_ref, rows_in, rebuilt_mine, mine, theirs, power_t, both_out, kept, tail, send, rows, rebuilt, sums, moved
):
    half, height, width = theirs.shape
    tokens, features = x.shape
    rank = left_ref.shape[1]
    chunks = range(width // LANES)
    left = left_ref[...]
    rows[...] = rows_in[...]

    @pl.loop(0, half // UNROLL)
    def _(step):
        for k in [step * UNROLL + u for u in range(UNROLL)]:
            gain_pass(2 * k + (1 - parity[0]), k, left, theirs, x, gain, rows, rebuilt, sums)

    first = row_mean(rows[2], features)
    second = row_mean(rows[3], features)
    rows[2] = rows[1] * rows[1] * second
    rows[3] = rows[0] * rows[2] - rows[1] * first

    def project(side, factors, source, target):
        def step(k, total):
            j = 2 * k + (parity[0] ^ side)
            columns = [pl.ds(pl.multiple_of(j * width + c * LANES, LANES), LANES) for c in chunks]
            gains = [jnp.broadcast_to(gain[:, columns[c]], (GROUP, LANES)) for c in chunks]
            groups = []
            for r in range(0, tokens, GROUP):
                group = slice(r, r + GROUP)
                inverse, slope, offset = rows[1, group], rows[2, group], rows[3, group]
                values = []
                for c in chunks:
                    lanes = slice(c * LANES, (c + 1) * LANES)
                    scaled = source[k, group, lanes] * gains[c]
                    value = scaled * inverse - x[group, columns[c]].astype(F32) * slope + offset
                    values.append(value.astype(BF16))
                    target[k, group, lanes] = values[-1]
                groups.append(jnp.concatenate(values, axis=1))
            block = jnp.concatenate(groups, axis=0)
            return total + lax.dot_general(block, factors[k, rank:, :], NT, preferred_element_type=F32)

        return step

    power = jnp.zeros((tokens, rank), F32)
    power = lax.fori_loop(0, half, project(0, mine, rebuilt_mine, kept), power, unroll=UNROLL)
    power = lax.fori_loop(0, half, project(1, theirs, rebuilt, moved), power, unroll=UNROLL).T
    power_t[...] = power
    gram = lax.dot_general(power, power, NT, precision=lax.Precision.HIGHEST, preferred_element_type=F32)
    side = rank // 2
    tail[...] = jnp.zeros_like(tail)
    packed = jnp.concatenate([gram[:side], gram[side:]], axis=1)
    per = width // LANES
    for q in range(side):
        tail[q // per : q // per + 1, (q % per) * LANES : (q % per + 1) * LANES] = packed[q : q + 1]
    high = power.astype(BF16)
    low = (power - high.astype(F32)).astype(BF16)
    both = jnp.concatenate([high, low], axis=0)
    both_out[...] = both
    feature_terms(both, moved, sums, tail, send)


def feature_terms(both, boundary, sums, tail, out):
    half, height, _ = out.shape
    rank = both.shape[0] // 2

    @pl.loop(0, half // UNROLL)
    def _(step):
        for k in [step * UNROLL + u for u in range(UNROLL)]:
            terms = jnp.dot(both, boundary[k], preferred_element_type=F32)
            out[k, :rank, :] = terms[:rank] + terms[rank:]
            out[k, rank : rank + 2, :] = sums[k, 0:2, :]
            out[k, rank + 2 :, :] = tail[: height - rank - 2]


def third_kernel(both, kept, sums, tail, keep):
    feature_terms(both[...], kept, sums, tail, keep)


def inverse_factor(gram):
    size = gram.shape[0]
    wide = 2 * size
    count = size // 8
    row = lax.broadcasted_iota(jnp.int32, (size, size), 0)
    col = lax.broadcasted_iota(jnp.int32, (size, size), 1)
    work = jnp.concatenate([gram, jnp.where(row == col, 1.0, 0.0).astype(F32)], axis=1)
    parts = [work[8 * i : 8 * i + 8] for i in range(count)]
    done = []
    for b in range(count):
        lines = [parts[b][r : r + 1] for r in range(8)]
        entry = {
            (i, j): jnp.broadcast_to(lines[i][:, 8 * b + j : 8 * b + j + 1], (1, wide))
            for i in range(8)
            for j in range(i + 1)
        }
        ratio, scale = {}, []
        for r in range(8):
            scale.append(1.0 / entry[r, r])
            for i in range(r + 1, 8):
                ratio[i, r] = entry[i, r] * scale[r]
            for i in range(r + 1, 8):
                for j in range(r + 1, i + 1):
                    entry[i, j] = entry[i, j] - ratio[i, r] * entry[j, r]
                lines[i] = lines[i] - ratio[i, r] * lines[r]
        done += [lines[r] * lax.rsqrt(entry[r, r]) for r in range(8)]
        solved = [None] * 8
        for r in reversed(range(8)):
            solved[r] = lines[r] * scale[r]
            for j in range(r + 1, 8):
                solved[r] = solved[r] - ratio[j, r] * solved[j]
        for i in range(b + 1, count):
            value = parts[i]
            for r in range(8):
                value = value - jnp.broadcast_to(parts[i][:, 8 * b + r : 8 * b + r + 1], (8, wide)) * solved[r]
            parts[i] = value
    return jnp.concatenate(done, axis=0)[:, size:]


def post_kernel(factor, terms, power_t, gain_out, bias_out, moved, square):
    rank, tokens = power_t.shape
    width = terms.shape[2]
    chunks = width // LANES
    half = rank // 2
    total = terms[0]
    for j in range(1, terms.shape[0]):
        total = total + terms[j]
    gain_out[...] = total[rank : rank + 1] * factor
    bias_out[...] = total[rank + 1 : rank + 2] * factor
    for q in range(half):
        line = rank + 2 + q // chunks
        start = (q % chunks) * LANES
        square[q : q + 1, :] = total[line : line + 1, start : start + LANES]
    packed = square[...]
    inverse = inverse_factor(jnp.concatenate([packed[:, :rank], packed[:, rank:]], axis=0))
    exact = dict(precision=lax.Precision.HIGHEST, preferred_element_type=F32)
    moved[:, :width] = jnp.dot(inverse, total[:rank], **exact).astype(BF16)
    moved[:, width:] = jnp.dot(inverse, power_t[...], **exact).astype(BF16)


def place_kernel(moved, left_out, right_out, sent):
    width = right_out.shape[1]
    copies = [
        pltpu.make_async_copy(moved.at[:, :width], right_out, sent.at[0]),
        pltpu.make_async_copy(moved.at[:, width:], left_out, sent.at[1]),
    ]
    for copy in copies:
        copy.start()
    for copy in copies:
        copy.wait()


def limit(mib):
    return pltpu.CompilerParams(vmem_limit_bytes=mib * 2**20)


def cost(mib):
    return pl.CostEstimate(flops=0, bytes_accessed=mib * 2**20, transcendentals=0)


def on_device(saved_input, norm_gain, left_in, right_in, basis):
    _, tokens, features = saved_input.shape
    width, rank = right_in.shape[1:]
    replicas = lax.axis_size("dp")
    half = replicas // 2
    chunks = width // LANES
    height = rank + 2 + -(-(rank // 2) // chunks)
    others = [(i, i ^ 1) for i in range(replicas)]
    groups = [[2 * k + c for k in range(half)] for c in range(2)]
    shape = jax.ShapeDtypeStruct

    x_hbm = pltpu.with_memory_space_constraint(saved_input[0], pltpu.HBM)
    own = jnp.concatenate([right_in[0].T, basis[0].T], axis=0)
    copies = jnp.broadcast_to(own[None], (half,) + own.shape)
    mine = lax.all_to_all(copies, "dp", 0, 0, tiled=True, axis_index_groups=groups)
    theirs = lax.ppermute(mine, "dp", others)
    parity = (lax.axis_index("dp") & 1).astype(jnp.int32).reshape(1)
    x, left, rows, rebuilt, sums = pl.pallas_call(
        first_kernel,
        out_shape=(
            shape((tokens, features), BF16),
            shape((tokens, rank), BF16),
            shape((4, tokens, LANES), F32),
            shape((half, tokens, width), F32),
            shape((half, 8, width), F32),
        ),
        in_specs=[SMEM, pl.BlockSpec(memory_space=pltpu.HBM), VMEM, VMEM, VMEM],
        out_specs=(VMEM,) * 5,
        scratch_shapes=[pltpu.SemaphoreType.DMA((replicas,))],
        compiler_params=limit(20),
        cost_estimate=cost(24),
    )(parity, x_hbm, norm_gain, left_in[0].T, mine)
    power_t, both, kept, tail, send = pl.pallas_call(
        second_kernel,
        out_shape=(
            shape((rank, tokens), F32),
            shape((2 * rank, tokens), BF16),
            shape((half, tokens, width), BF16),
            shape((8, width), F32),
            shape((half, height, width), F32),
        ),
        in_specs=[SMEM] + [VMEM] * 7,
        out_specs=(VMEM,) * 5,
        scratch_shapes=[
            pltpu.VMEM((4, tokens, LANES), F32),
            pltpu.VMEM((half, tokens, width), F32),
            pltpu.VMEM((half, 8, width), F32),
            pltpu.VMEM((half, tokens, width), BF16),
        ],
        compiler_params=limit(32),
    )(parity, x, norm_gain, left, rows, rebuilt, mine, theirs)
    other = lax.ppermute(send, "dp", others)
    keep = pl.pallas_call(
        third_kernel,
        out_shape=shape((half, height, width), F32),
        in_specs=[VMEM] * 4,
        out_specs=VMEM,
        compiler_params=limit(12),
        cost_estimate=cost(12),
    )(both, kept, sums, tail)
    terms = lax.all_to_all(keep + other, "dp", 0, 0, tiled=True, axis_index_groups=groups)

    factor = float(1.0 / (tokens * replicas) ** 0.5)
    gain_grad, bias_grad, moved = pl.pallas_call(
        lambda *refs: post_kernel(factor, *refs),
        out_shape=(shape((1, width), F32), shape((1, width), F32), shape((rank, width + tokens), BF16)),
        in_specs=[VMEM, VMEM],
        out_specs=(VMEM,) * 3,
        scratch_shapes=[pltpu.VMEM((rank // 2, LANES), F32)],
        compiler_params=limit(16),
    )(terms, power_t)
    sections = lax.axis_size("section")
    moved = lax.ppermute(moved, "section", [(i, i - 1) for i in range(1, sections)])
    left_out, right_out = pl.pallas_call(
        place_kernel,
        out_shape=(shape((rank, tokens), BF16), shape((rank, width), BF16)),
        in_specs=[VMEM],
        out_specs=(pl.BlockSpec(memory_space=pltpu.HBM),) * 2,
        scratch_shapes=[pltpu.SemaphoreType.DMA((2,))],
        compiler_params=limit(4),
    )(moved)
    return gain_grad, bias_grad, left_out.T[None], right_out.T[None]


def solution(mesh):
    placed = (
        P("section", "dp", None),
        P("section", None),
        P("section", "dp", None),
        P("section", "dp", None),
        P("section", "dp", None),
    )
    return jax.shard_map(
        on_device,
        mesh=mesh,
        in_specs=placed,
        out_specs=(
            P("section", "dp"),
            P("section", "dp"),
            P("section", "dp", None),
            P("section", "dp", None),
        ),
        check_vma=False,
    )
```

```python
import jax
import jax.numpy as jnp
from jax import lax
from jax.experimental import pallas as pl
from jax.experimental.pallas import tpu as pltpu
from jax.sharding import PartitionSpec as P

LANES = 128
GROUP = 16
UNROLL = 4
F32 = jnp.float32
BF16 = jnp.bfloat16
NT = (((1,), (1,)), ((), ()))
EXACT = dict(precision=lax.Precision.HIGHEST, preferred_element_type=F32)
VMEM = pl.BlockSpec(memory_space=pltpu.VMEM)
SMEM = pl.BlockSpec(memory_space=pltpu.SMEM)


def fold(value):
    return value[:8] + value[8:]


def gain_pass(j, k, left, factors, x, gain, rows, rebuilt, sums, plain=True, normal=True):
    tokens, width = rebuilt.shape[1:]
    rank = left.shape[1]
    chunks = range(width // LANES)
    columns = [pl.ds(pl.multiple_of(j * width + c * LANES, LANES), LANES) for c in chunks]
    gains = [jnp.broadcast_to(gain[:, columns[c]], (GROUP, LANES)) for c in chunks]
    products = [jnp.zeros((8, LANES), F32) for _ in chunks]
    bare = [jnp.zeros((8, LANES), F32) for _ in chunks]
    if plain:
        rebuilt[k] = jnp.dot(left, factors[k, :rank, :], preferred_element_type=F32)
    for r in range(0, tokens, GROUP):
        group = slice(r, r + GROUP)
        if normal:
            mean, inverse, second = rows[0, group], rows[1, group], rows[3, group]
        if plain:
            first = rows[2, group]
        for c in chunks:
            part = rebuilt[k, group, c * LANES : (c + 1) * LANES]
            scaled = part * gains[c]
            if plain:
                first = first + scaled
                bare[c] = bare[c] + fold(part)
            if normal:
                normed = (x[group, columns[c]].astype(F32) - mean) * inverse
                second = second + scaled * normed
                products[c] = products[c] + fold(part * normed)
        if plain:
            rows[2, group] = first
        if normal:
            rows[3, group] = second
    for c in chunks:
        lanes = slice(c * LANES, (c + 1) * LANES)
        if normal:
            sums[k, 0:1, lanes] = jnp.sum(products[c], axis=0, keepdims=True)
        if plain:
            sums[k, 1:2, lanes] = jnp.sum(bare[c], axis=0, keepdims=True)


def row_mean(total, features):
    return jnp.broadcast_to(jnp.sum(total, axis=1, keepdims=True) * (1.0 / features), total.shape)


def first_kernel(parity, x_hbm, gain, left_t, mine, x, left_out, rows, rebuilt, sums, arrived):
    half, _, width = mine.shape
    tokens, features = x.shape
    blocks = 2 * half
    chunks = range(width // LANES)

    def fetch(j):
        columns = pl.ds(pl.multiple_of(j * width, LANES), width)
        return pltpu.make_async_copy(x_hbm.at[:, columns], x.at[:, columns], arrived.at[j])

    @pl.loop(0, blocks)
    def _(j):
        fetch(j).start()

    left_out[...] = left_t[...].astype(F32).T.astype(BF16)
    left = left_out[...]
    rows[...] = jnp.zeros_like(rows)

    for j in range(UNROLL):
        fetch(j).wait()
    for r in range(0, tokens, GROUP):
        group = slice(r, r + GROUP)
        total = x[group, :LANES].astype(F32)
        for c in chunks[1:]:
            total = total + x[group, c * LANES : (c + 1) * LANES].astype(F32)
        rows[0, group] = row_mean(total, width)

    @pl.loop(0, blocks // UNROLL)
    def _(step):
        @pl.when(step > 0)
        def _():
            for u in range(UNROLL):
                fetch(step * UNROLL + u).wait()

        for r in range(0, tokens, GROUP):
            group = slice(r, r + GROUP)
            base, total, squares = rows[0, group], rows[1, group], rows[3, group]
            for u in range(UNROLL):
                for c in chunks:
                    start = (step * UNROLL + u) * width + c * LANES
                    center = x[group, pl.ds(pl.multiple_of(start, LANES), LANES)].astype(F32) - base
                    total = total + center
                    squares = squares + center * center
            rows[1, group] = total
            rows[3, group] = squares
        for k in [step * UNROLL // 2 + u for u in range(UNROLL // 2)]:
            gain_pass(2 * k + parity[0], k, left, mine, x, gain, rows, rebuilt, sums, normal=False)

    shift = row_mean(rows[1], features)
    variance = jnp.maximum(row_mean(rows[3], features) - shift * shift, 0.0)
    rows[0] = rows[0] + shift
    rows[1] = lax.rsqrt(variance + 1e-05)
    rows[3] = jnp.zeros((tokens, LANES), F32)

    @pl.loop(0, half // UNROLL)
    def _(step):
        for k in [step * UNROLL + u for u in range(UNROLL)]:
            gain_pass(2 * k + parity[0], k, left, mine, x, gain, rows, rebuilt, sums, plain=False)


def second_kernel(
    parity, x, gain, left_ref, rows_in, rebuilt_mine, mine, theirs, power_t, kept, packed, send, rows, rebuilt, sums, moved, tail
):
    half, height, width = theirs.shape
    tokens, features = x.shape
    rank = left_ref.shape[1]
    chunks = range(width // LANES)
    left = left_ref[...]
    rows[...] = rows_in[...]

    def mixing(k, total):
        terms = []
        for side, factors in enumerate((mine, theirs)):
            start = (2 * k + (parity[0] ^ side)) * width
            scaled = factors[k, :rank, :].astype(F32) * gain[:, pl.ds(pl.multiple_of(start, LANES), width)]
            terms.append(lax.dot_general(factors[k, rank:, :], scaled.astype(BF16), NT, preferred_element_type=F32))
        return total + (terms[0] + terms[1])

    mixed = lax.fori_loop(0, half, mixing, jnp.zeros((rank, rank), F32), unroll=UNROLL)
    near = lax.dot_general(mixed, mixed, NT, **EXACT)
    row = lax.broadcasted_iota(jnp.int32, near.shape, 0)
    col = lax.broadcasted_iota(jnp.int32, near.shape, 1)
    level = jnp.sum(mixed * mixed) * (1e-06 / rank) + 1e-08
    basis_change = inverse_factor(near + jnp.where(row == col, level, 0.0))

    @pl.loop(0, half // UNROLL)
    def _(step):
        for k in [step * UNROLL + u for u in range(UNROLL)]:
            gain_pass(2 * k + (1 - parity[0]), k, left, theirs, x, gain, rows, rebuilt, sums)

    first = row_mean(rows[2], features)
    second = row_mean(rows[3], features)
    rows[2] = rows[1] * rows[1] * second
    rows[3] = rows[0] * rows[2] - rows[1] * first

    def project(side, factors, source, target):
        def step(k, total):
            j = 2 * k + (parity[0] ^ side)
            columns = [pl.ds(pl.multiple_of(j * width + c * LANES, LANES), LANES) for c in chunks]
            gains = [jnp.broadcast_to(gain[:, columns[c]], (GROUP, LANES)) for c in chunks]
            groups = []
            for r in range(0, tokens, GROUP):
                group = slice(r, r + GROUP)
                inverse, slope, offset = rows[1, group], rows[2, group], rows[3, group]
                values = []
                for c in chunks:
                    lanes = slice(c * LANES, (c + 1) * LANES)
                    scaled = source[k, group, lanes] * gains[c]
                    value = scaled * inverse - x[group, columns[c]].astype(F32) * slope + offset
                    values.append(value.astype(BF16))
                    target[k, group, lanes] = values[-1]
                groups.append(jnp.concatenate(values, axis=1))
            block = jnp.concatenate(groups, axis=0)
            return total + lax.dot_general(block, factors[k, rank:, :], NT, preferred_element_type=F32)

        return step

    power = jnp.zeros((tokens, rank), F32)
    power = lax.fori_loop(0, half, project(0, mine, rebuilt_mine, kept), power, unroll=UNROLL)
    power = lax.fori_loop(0, half, project(1, theirs, rebuilt, moved), power, unroll=UNROLL)
    power = lax.dot_general(basis_change, power, NT, **EXACT)
    power_t[...] = power
    pack(lax.dot_general(power, power, NT, **EXACT), packed)
    high = power.astype(BF16)
    split_gram(packed[0:4, :], tail)

    @pl.loop(0, half // UNROLL)
    def _(step):
        for k in [step * UNROLL + u for u in range(UNROLL)]:
            terms = jnp.dot(high, moved[k], preferred_element_type=F32)
            send[k, :rank, :] = terms.astype(BF16)
            split_sums(sums[k, 0:2, :], tail)
            send[k, rank:, :] = tail[...].astype(BF16)


def split(value, count):
    terms = []
    for _ in range(count):
        terms.append(value.astype(BF16).astype(F32))
        value = value - terms[-1]
    return terms


def split_sums(value, tail):
    for i, term in enumerate(split(value, 2)):
        tail[2 * i : 2 * i + 2, :] = term


def split_gram(value, tail):
    for i, term in enumerate(split(value, 3)):
        tail[4 + 4 * i : 8 + 4 * i, :] = term


def pack(gram, packed):
    size = gram.shape[0]
    half, quarter = size // 2, size // 4
    per = packed.shape[1] // LANES
    corner = gram[half:, half:]
    upper = jnp.concatenate([gram[:quarter], gram[quarter:half]], axis=1)
    lower = jnp.concatenate([corner[8 * i : 8 * i + 8] for i in range(half // 8)], axis=1)
    packed[...] = jnp.zeros_like(packed)
    for q in range(quarter + 8):
        line = upper[q : q + 1] if q < quarter else lower[q - quarter : q - quarter + 1]
        packed[q // per : q // per + 1, (q % per) * LANES : (q % per + 1) * LANES] = line


def unpack(packed, square):
    lines = square.shape[0]
    per = packed.shape[1] // LANES
    quarter = lines - 8
    half = 2 * quarter
    for q in range(lines):
        square[q : q + 1, :] = packed[q // per : q // per + 1, (q % per) * LANES : (q % per + 1) * LANES]
    upper = jnp.concatenate([square[:quarter, : 2 * half], square[:quarter, 2 * half :]], axis=0)
    corner = jnp.concatenate([square[quarter:, half * i : half * (i + 1)] for i in range(half // 8)], axis=0)
    return jnp.concatenate([upper, jnp.concatenate([upper[:, half:].T, corner], axis=1)], axis=0)


def third_kernel(power_t, kept, keep):
    high = power_t[...].astype(BF16)

    @pl.loop(0, keep.shape[0] // UNROLL)
    def _(step):
        for k in [step * UNROLL + u for u in range(UNROLL)]:
            keep[k] = jnp.dot(high, kept[k], preferred_element_type=F32)


def pair_kernel(keep, packed, sums, other, out, tail):
    half, rank, _ = keep.shape
    theirs = other[0, rank:, :].astype(F32)
    split_gram(packed[0:4, :] + (theirs[4:8] + (theirs[8:12] + theirs[12:16])), tail)

    @pl.loop(0, half // UNROLL)
    def _(step):
        for k in [step * UNROLL + u for u in range(UNROLL)]:
            out[k, :rank, :] = (keep[k] + other[k, :rank, :].astype(F32)).astype(BF16)
            theirs = other[k, rank:, :].astype(F32)
            split_sums(sums[k, 0:2, :] + (theirs[0:2] + theirs[2:4]), tail)
            out[k, rank:, :] = tail[...].astype(BF16)


def inverse_factor(gram):
    size = gram.shape[0]
    wide = 2 * size
    count = size // 8
    row = lax.broadcasted_iota(jnp.int32, (size, size), 0)
    col = lax.broadcasted_iota(jnp.int32, (size, size), 1)
    work = jnp.concatenate([gram, jnp.where(row == col, 1.0, 0.0).astype(F32)], axis=1)
    parts = [work[8 * i : 8 * i + 8] for i in range(count)]
    done = []
    for b in range(count):
        lines = [parts[b][r : r + 1] for r in range(8)]
        entry = {
            (i, j): jnp.broadcast_to(lines[i][:, 8 * b + j : 8 * b + j + 1], (1, wide))
            for i in range(8)
            for j in range(i + 1)
        }
        ratio, scale = {}, []
        for r in range(8):
            scale.append(1.0 / entry[r, r])
            for i in range(r + 1, 8):
                ratio[i, r] = entry[i, r] * scale[r]
            for i in range(r + 1, 8):
                for j in range(r + 1, i + 1):
                    entry[i, j] = entry[i, j] - ratio[i, r] * entry[j, r]
                lines[i] = lines[i] - ratio[i, r] * lines[r]
        done += [lines[r] * lax.rsqrt(entry[r, r]) for r in range(8)]
        solved = [None] * 8
        for r in reversed(range(8)):
            solved[r] = lines[r] * scale[r]
            for j in range(r + 1, 8):
                solved[r] = solved[r] - ratio[j, r] * solved[j]
        for i in range(b + 1, count):
            value = parts[i]
            for r in range(8):
                value = value - jnp.broadcast_to(parts[i][:, 8 * b + r : 8 * b + r + 1], (8, wide)) * solved[r]
            parts[i] = value
    return jnp.concatenate(done, axis=0)[:, size:]


def post_kernel(factor, terms, power_t, gain_out, bias_out, moved, square):
    rank, tokens = power_t.shape
    width = terms.shape[2]
    total = terms[0].astype(F32)
    for j in range(1, terms.shape[0]):
        total = total + terms[j].astype(F32)
    extra = total[rank:]
    gain_out[...] = (extra[0:1] + extra[2:3]) * factor
    bias_out[...] = (extra[1:2] + extra[3:4]) * factor
    inverse = inverse_factor(unpack(extra[4:8] + (extra[8:12] + extra[12:16]), square))
    moved[:, :width] = jnp.dot(inverse, total[:rank], **EXACT).astype(BF16)
    moved[:, width:] = jnp.dot(inverse, power_t[...], **EXACT).astype(BF16)


def place_kernel(moved, left_out, right_out, sent):
    width = right_out.shape[1]
    copies = [
        pltpu.make_async_copy(moved.at[:, :width], right_out, sent.at[0]),
        pltpu.make_async_copy(moved.at[:, width:], left_out, sent.at[1]),
    ]
    for copy in copies:
        copy.start()
    for copy in copies:
        copy.wait()


def limit(mib):
    return pltpu.CompilerParams(vmem_limit_bytes=mib * 2**20)


def cost(mib):
    return pl.CostEstimate(flops=0, bytes_accessed=mib * 2**20, transcendentals=0)


def on_device(saved_input, norm_gain, left_in, right_in, basis):
    _, tokens, features = saved_input.shape
    width, rank = right_in.shape[1:]
    replicas = lax.axis_size("dp")
    half = replicas // 2
    height = rank + 16
    others = [(i, i ^ 1) for i in range(replicas)]
    groups = [[2 * k + c for k in range(half)] for c in range(2)]
    shape = jax.ShapeDtypeStruct

    x_hbm = pltpu.with_memory_space_constraint(saved_input[0], pltpu.HBM)
    own = jnp.concatenate([right_in[0].T, basis[0].T], axis=0)
    copies = jnp.broadcast_to(own[None], (half,) + own.shape)
    mine = lax.all_to_all(copies, "dp", 0, 0, tiled=True, axis_index_groups=groups)
    theirs = lax.ppermute(mine, "dp", others)
    parity = (lax.axis_index("dp") & 1).astype(jnp.int32).reshape(1)
    x, left, rows, rebuilt, sums = pl.pallas_call(
        first_kernel,
        out_shape=(
            shape((tokens, features), BF16),
            shape((tokens, rank), BF16),
            shape((4, tokens, LANES), F32),
            shape((half, tokens, width), F32),
            shape((half, 8, width), F32),
        ),
        in_specs=[SMEM, pl.BlockSpec(memory_space=pltpu.HBM), VMEM, VMEM, VMEM],
        out_specs=(VMEM,) * 5,
        scratch_shapes=[pltpu.SemaphoreType.DMA((replicas,))],
        compiler_params=limit(20),
        cost_estimate=cost(24),
    )(parity, x_hbm, norm_gain, left_in[0].T, mine)
    power_t, kept, packed, send = pl.pallas_call(
        second_kernel,
        out_shape=(
            shape((rank, tokens), F32),
            shape((half, tokens, width), BF16),
            shape((8, width), F32),
            shape((half, height, width), BF16),
        ),
        in_specs=[SMEM] + [VMEM] * 7,
        out_specs=(VMEM,) * 4,
        scratch_shapes=[
            pltpu.VMEM((4, tokens, LANES), F32),
            pltpu.VMEM((half, tokens, width), F32),
            pltpu.VMEM((half, 8, width), F32),
            pltpu.VMEM((half, tokens, width), BF16),
            pltpu.VMEM((16, width), F32),
        ],
        compiler_params=limit(32),
    )(parity, x, norm_gain, left, rows, rebuilt, mine, theirs)
    other = lax.ppermute(send, "dp", others)
    keep = pl.pallas_call(
        third_kernel,
        out_shape=shape((half, rank, width), F32),
        in_specs=[VMEM] * 2,
        out_specs=VMEM,
        compiler_params=limit(12),
        cost_estimate=cost(12),
    )(power_t, kept)
    payload = pl.pallas_call(
        pair_kernel,
        out_shape=shape((half, height, width), BF16),
        in_specs=[VMEM] * 4,
        out_specs=VMEM,
        scratch_shapes=[pltpu.VMEM((16, width), F32)],
        compiler_params=limit(12),
    )(keep, packed, sums, other)
    terms = lax.all_to_all(payload, "dp", 0, 0, tiled=True, axis_index_groups=groups)

    factor = float(1.0 / (tokens * replicas) ** 0.5)
    gain_grad, bias_grad, moved = pl.pallas_call(
        lambda *refs: post_kernel(factor, *refs),
        out_shape=(shape((1, width), F32), shape((1, width), F32), shape((rank, width + tokens), BF16)),
        in_specs=[VMEM, VMEM],
        out_specs=(VMEM,) * 3,
        scratch_shapes=[pltpu.VMEM((24, LANES), F32)],
        compiler_params=limit(16),
    )(terms, power_t)
    sections = lax.axis_size("section")
    moved = lax.ppermute(moved, "section", [(i, i - 1) for i in range(1, sections)])
    left_out, right_out = pl.pallas_call(
        place_kernel,
        out_shape=(shape((rank, tokens), BF16), shape((rank, width), BF16)),
        in_specs=[VMEM],
        out_specs=(pl.BlockSpec(memory_space=pltpu.HBM),) * 2,
        scratch_shapes=[pltpu.SemaphoreType.DMA((2,))],
        compiler_params=limit(4),
    )(moved)
    return gain_grad, bias_grad, left_out.T[None], right_out.T[None]


def solution(mesh):
    placed = (
        P("section", "dp", None),
        P("section", None),
        P("section", "dp", None),
        P("section", "dp", None),
        P("section", "dp", None),
    )
    return jax.shard_map(
        on_device,
        mesh=mesh,
        in_specs=placed,
        out_specs=(
            P("section", "dp"),
            P("section", "dp"),
            P("section", "dp", None),
            P("section", "dp", None),
        ),
        check_vma=False,
    )
```

```python
import jax
import jax.numpy as jnp
from jax import lax
from jax.experimental import pallas as pl
from jax.experimental.pallas import tpu as pltpu
from jax.sharding import PartitionSpec as P

LANES = 128
GROUP = 16
UNROLL = 8
FETCH = 2
F32 = jnp.float32
BF16 = jnp.bfloat16
NT = (((1,), (1,)), ((), ()))
EXACT = dict(precision=lax.Precision.HIGHEST, preferred_element_type=F32)
VMEM = pl.BlockSpec(memory_space=pltpu.VMEM)
SMEM = pl.BlockSpec(memory_space=pltpu.SMEM)


def fold(value):
    return value[:8] + value[8:]


def gain_pass(j, k, left, factors, x, gain, rows, rebuilt, sums, plain=True, normal=True):
    tokens, width = rebuilt.shape[1:]
    rank = left.shape[1]
    chunks = range(width // LANES)
    columns = [pl.ds(pl.multiple_of(j * width + c * LANES, LANES), LANES) for c in chunks]
    gains = [jnp.broadcast_to(gain[:, columns[c]], (GROUP, LANES)) for c in chunks]
    products = [jnp.zeros((8, LANES), F32) for _ in chunks]
    bare = [jnp.zeros((8, LANES), F32) for _ in chunks]
    if plain:
        rebuilt[k] = jnp.dot(left, factors[k, :rank, :], preferred_element_type=F32)
    for r in range(0, tokens, GROUP):
        group = slice(r, r + GROUP)
        if normal:
            mean, inverse, second = rows[0, group], rows[1, group], rows[3, group]
        if plain:
            first = rows[2, group]
        for c in chunks:
            part = rebuilt[k, group, c * LANES : (c + 1) * LANES]
            scaled = part * gains[c]
            if plain:
                first = first + scaled
                bare[c] = bare[c] + fold(part)
            if normal:
                normed = (x[group, columns[c]].astype(F32) - mean) * inverse
                second = second + scaled * normed
                products[c] = products[c] + fold(part * normed)
        if plain:
            rows[2, group] = first
        if normal:
            rows[3, group] = second
    for c in chunks:
        lanes = slice(c * LANES, (c + 1) * LANES)
        if normal:
            sums[k, 0:1, lanes] = jnp.sum(products[c], axis=0, keepdims=True)
        if plain:
            sums[k, 1:2, lanes] = jnp.sum(bare[c], axis=0, keepdims=True)


def row_mean(total, features):
    return jnp.broadcast_to(jnp.sum(total, axis=1, keepdims=True) * (1.0 / features), total.shape)


def first_kernel(parity, x_hbm, gain, left_t, mine, x, left_out, rows, rebuilt, sums, arrived):
    half, _, width = mine.shape
    tokens, features = x.shape
    blocks = 2 * half
    chunks = range(width // LANES)

    def fetch(j):
        columns = pl.ds(pl.multiple_of(j * width, LANES), width)
        return pltpu.make_async_copy(x_hbm.at[:, columns], x.at[:, columns], arrived.at[j])

    @pl.loop(0, blocks)
    def _(j):
        fetch(j).start()

    left_out[...] = left_t[...].astype(F32).T.astype(BF16)
    left = left_out[...]
    rows[...] = jnp.zeros_like(rows)

    @pl.loop(0, half // UNROLL)
    def _(step):
        for k in [step * UNROLL + u for u in range(UNROLL)]:
            gain_pass(2 * k + parity[0], k, left, mine, x, gain, rows, rebuilt, sums, normal=False)

    for j in range(FETCH):
        fetch(j).wait()
    for r in range(0, tokens, GROUP):
        group = slice(r, r + GROUP)
        total = x[group, :LANES].astype(F32)
        for c in chunks[1:]:
            total = total + x[group, c * LANES : (c + 1) * LANES].astype(F32)
        rows[0, group] = row_mean(total, width)

    @pl.loop(0, blocks // FETCH)
    def _(step):
        @pl.when(step > 0)
        def _():
            for u in range(FETCH):
                fetch(step * FETCH + u).wait()

        for r in range(0, tokens, GROUP):
            group = slice(r, r + GROUP)
            base, total, squares = rows[0, group], rows[1, group], rows[3, group]
            for u in range(FETCH):
                for c in chunks:
                    start = (step * FETCH + u) * width + c * LANES
                    center = x[group, pl.ds(pl.multiple_of(start, LANES), LANES)].astype(F32) - base
                    total = total + center
                    squares = squares + center * center
            rows[1, group] = total
            rows[3, group] = squares

    shift = row_mean(rows[1], features)
    variance = jnp.maximum(row_mean(rows[3], features) - shift * shift, 0.0)
    rows[0] = rows[0] + shift
    rows[1] = lax.rsqrt(variance + 1e-05)
    rows[3] = jnp.zeros((tokens, LANES), F32)

    @pl.loop(0, half // UNROLL)
    def _(step):
        for k in [step * UNROLL + u for u in range(UNROLL)]:
            gain_pass(2 * k + parity[0], k, left, mine, x, gain, rows, rebuilt, sums, plain=False)


def second_kernel(
    parity, x, gain, left_ref, rows_in, rebuilt_mine, mine, theirs, power_t, kept, packed, send, rows, rebuilt, sums, moved, tail
):
    half, height, width = theirs.shape
    tokens, features = x.shape
    rank = left_ref.shape[1]
    chunks = range(width // LANES)
    left = left_ref[...]
    rows[...] = rows_in[...]

    def mixing(k, total):
        terms = []
        for side, factors in enumerate((mine, theirs)):
            start = (2 * k + (parity[0] ^ side)) * width
            scaled = factors[k, :rank, :] * gain[:, pl.ds(pl.multiple_of(start, LANES), width)].astype(BF16)
            terms.append(scaled)
        basis = jnp.concatenate([mine[k, rank:, :], theirs[k, rank:, :]], axis=0)
        both = lax.dot_general(basis, jnp.concatenate(terms, axis=0), NT, preferred_element_type=F32)
        return total + (both[:rank, :rank] + both[rank:, rank:])

    mixed = lax.fori_loop(0, half, mixing, jnp.zeros((rank, rank), F32), unroll=UNROLL)
    near = lax.dot_general(mixed, mixed, NT, **EXACT)
    row = lax.broadcasted_iota(jnp.int32, near.shape, 0)
    col = lax.broadcasted_iota(jnp.int32, near.shape, 1)
    level = jnp.sum(mixed * mixed) * (1e-06 / rank) + 1e-08
    basis_change = inverse_factor(near + jnp.where(row == col, level, 0.0))

    @pl.loop(0, half // UNROLL)
    def _(step):
        for k in [step * UNROLL + u for u in range(UNROLL)]:
            gain_pass(2 * k + (1 - parity[0]), k, left, theirs, x, gain, rows, rebuilt, sums)

    first = row_mean(rows[2], features)
    second = row_mean(rows[3], features)
    rows[2] = rows[1] * rows[1] * second
    rows[3] = rows[0] * rows[2] - rows[1] * first

    def project(side, factors, source, target):
        def step(k, total):
            j = 2 * k + (parity[0] ^ side)
            columns = [pl.ds(pl.multiple_of(j * width + c * LANES, LANES), LANES) for c in chunks]
            gains = [jnp.broadcast_to(gain[:, columns[c]], (GROUP, LANES)) for c in chunks]
            groups = []
            for r in range(0, tokens, GROUP):
                group = slice(r, r + GROUP)
                inverse, slope, offset = rows[1, group], rows[2, group], rows[3, group]
                values = []
                for c in chunks:
                    lanes = slice(c * LANES, (c + 1) * LANES)
                    scaled = source[k, group, lanes] * gains[c]
                    value = scaled * inverse - x[group, columns[c]].astype(F32) * slope + offset
                    values.append(value.astype(BF16))
                    target[k, group, lanes] = values[-1]
                groups.append(jnp.concatenate(values, axis=1))
            block = jnp.concatenate(groups, axis=0)
            return total + lax.dot_general(block, factors[k, rank:, :], NT, preferred_element_type=F32)

        return step

    power = jnp.zeros((tokens, rank), F32)
    power = lax.fori_loop(0, half, project(0, mine, rebuilt_mine, kept), power, unroll=UNROLL)
    power = lax.fori_loop(0, half, project(1, theirs, rebuilt, moved), power, unroll=UNROLL)
    power = lax.dot_general(basis_change, power, NT, **EXACT)
    power_t[...] = power
    pack(lax.dot_general(power, power, NT, **EXACT), packed)
    high = power.astype(BF16)
    split_gram(packed[0:4, :], tail)

    @pl.loop(0, half // UNROLL)
    def _(step):
        for k in [step * UNROLL + u for u in range(UNROLL)]:
            terms = jnp.dot(high, moved[k], preferred_element_type=F32)
            send[k, :rank, :] = terms.astype(BF16)
            split_sums(sums[k, 0:2, :], tail)
            send[k, rank:, :] = tail[...].astype(BF16)


def split(value, count):
    terms = []
    for _ in range(count):
        terms.append(value.astype(BF16).astype(F32))
        value = value - terms[-1]
    return terms


def split_sums(value, tail):
    for i, term in enumerate(split(value, 2)):
        tail[2 * i : 2 * i + 2, :] = term


def split_gram(value, tail):
    for i, term in enumerate(split(value, 3)):
        tail[4 + 4 * i : 8 + 4 * i, :] = term


def pack(gram, packed):
    size = gram.shape[0]
    half, quarter = size // 2, size // 4
    per = packed.shape[1] // LANES
    corner = gram[half:, half:]
    upper = jnp.concatenate([gram[:quarter], gram[quarter:half]], axis=1)
    lower = jnp.concatenate([corner[8 * i : 8 * i + 8] for i in range(half // 8)], axis=1)
    packed[...] = jnp.zeros_like(packed)
    for q in range(quarter + 8):
        line = upper[q : q + 1] if q < quarter else lower[q - quarter : q - quarter + 1]
        packed[q // per : q // per + 1, (q % per) * LANES : (q % per + 1) * LANES] = line


def unpack(packed, square):
    lines = square.shape[0]
    per = packed.shape[1] // LANES
    quarter = lines - 8
    half = 2 * quarter
    for q in range(lines):
        square[q : q + 1, :] = packed[q // per : q // per + 1, (q % per) * LANES : (q % per + 1) * LANES]
    upper = jnp.concatenate([square[:quarter, : 2 * half], square[:quarter, 2 * half :]], axis=0)
    corner = jnp.concatenate([square[quarter:, half * i : half * (i + 1)] for i in range(half // 8)], axis=0)
    return jnp.concatenate([upper, jnp.concatenate([upper[:, half:].T, corner], axis=1)], axis=0)


def third_kernel(power_t, kept, keep):
    high = power_t[...].astype(BF16)

    @pl.loop(0, keep.shape[0] // UNROLL)
    def _(step):
        for k in [step * UNROLL + u for u in range(UNROLL)]:
            keep[k] = jnp.dot(high, kept[k], preferred_element_type=F32)


def pair_kernel(keep, packed, sums, other, out, tail):
    half, rank, _ = keep.shape
    theirs = other[0, rank:, :].astype(F32)
    split_gram(packed[0:4, :] + (theirs[4:8] + (theirs[8:12] + theirs[12:16])), tail)

    @pl.loop(0, half // UNROLL)
    def _(step):
        for k in [step * UNROLL + u for u in range(UNROLL)]:
            out[k, :rank, :] = (keep[k] + other[k, :rank, :].astype(F32)).astype(BF16)
            theirs = other[k, rank:, :].astype(F32)
            split_sums(sums[k, 0:2, :] + (theirs[0:2] + theirs[2:4]), tail)
            out[k, rank:, :] = tail[...].astype(BF16)


def inverse_factor(gram):
    size = gram.shape[0]
    wide = 2 * size
    count = size // 8
    row = lax.broadcasted_iota(jnp.int32, (size, size), 0)
    col = lax.broadcasted_iota(jnp.int32, (size, size), 1)
    work = jnp.concatenate([gram, jnp.where(row == col, 1.0, 0.0).astype(F32)], axis=1)
    parts = [work[8 * i : 8 * i + 8] for i in range(count)]
    done = []
    for b in range(count):
        lines = [parts[b][r : r + 1] for r in range(8)]
        entry = {
            (i, j): jnp.broadcast_to(lines[i][:, 8 * b + j : 8 * b + j + 1], (1, wide))
            for i in range(8)
            for j in range(i + 1)
        }
        ratio, scale = {}, []
        for r in range(8):
            scale.append(1.0 / entry[r, r])
            for i in range(r + 1, 8):
                ratio[i, r] = entry[i, r] * scale[r]
            for i in range(r + 1, 8):
                for j in range(r + 1, i + 1):
                    entry[i, j] = entry[i, j] - ratio[i, r] * entry[j, r]
                lines[i] = lines[i] - ratio[i, r] * lines[r]
        done += [lines[r] * lax.rsqrt(entry[r, r]) for r in range(8)]
        solved = [None] * 8
        for r in reversed(range(8)):
            solved[r] = lines[r] * scale[r]
            for j in range(r + 1, 8):
                solved[r] = solved[r] - ratio[j, r] * solved[j]
        for i in range(b + 1, count):
            value = parts[i]
            for r in range(8):
                value = value - jnp.broadcast_to(parts[i][:, 8 * b + r : 8 * b + r + 1], (8, wide)) * solved[r]
            parts[i] = value
    return jnp.concatenate(done, axis=0)[:, size:]


def post_kernel(factor, terms, power_t, gain_out, bias_out, moved, square):
    rank, tokens = power_t.shape
    width = terms.shape[2]
    total = terms[0].astype(F32)
    for j in range(1, terms.shape[0]):
        total = total + terms[j].astype(F32)
    extra = total[rank:]
    gain_out[...] = (extra[0:1] + extra[2:3]) * factor
    bias_out[...] = (extra[1:2] + extra[3:4]) * factor
    inverse = inverse_factor(unpack(extra[4:8] + (extra[8:12] + extra[12:16]), square))
    moved[:, :width] = jnp.dot(inverse, total[:rank], **EXACT).astype(BF16)
    moved[:, width:] = jnp.dot(inverse, power_t[...], **EXACT).astype(BF16)


def place_kernel(moved, left_out, right_out, sent):
    width = right_out.shape[1]
    copies = [
        pltpu.make_async_copy(moved.at[:, :width], right_out, sent.at[0]),
        pltpu.make_async_copy(moved.at[:, width:], left_out, sent.at[1]),
    ]
    for copy in copies:
        copy.start()
    for copy in copies:
        copy.wait()


def limit(mib):
    return pltpu.CompilerParams(vmem_limit_bytes=mib * 2**20)


def cost(mib):
    return pl.CostEstimate(flops=0, bytes_accessed=mib * 2**20, transcendentals=0)


def on_device(saved_input, norm_gain, left_in, right_in, basis):
    _, tokens, features = saved_input.shape
    width, rank = right_in.shape[1:]
    replicas = lax.axis_size("dp")
    half = replicas // 2
    height = rank + 16
    others = [(i, i ^ 1) for i in range(replicas)]
    groups = [[2 * k + c for k in range(half)] for c in range(2)]
    shape = jax.ShapeDtypeStruct

    x_hbm = pltpu.with_memory_space_constraint(saved_input[0], pltpu.HBM)
    own = jnp.concatenate([right_in[0].T, basis[0].T], axis=0)
    copies = jnp.broadcast_to(own[None], (half,) + own.shape)
    mine = lax.all_to_all(copies, "dp", 0, 0, tiled=True, axis_index_groups=groups)
    theirs = lax.ppermute(mine, "dp", others)
    parity = (lax.axis_index("dp") & 1).astype(jnp.int32).reshape(1)
    x, left, rows, rebuilt, sums = pl.pallas_call(
        first_kernel,
        out_shape=(
            shape((tokens, features), BF16),
            shape((tokens, rank), BF16),
            shape((4, tokens, LANES), F32),
            shape((half, tokens, width), F32),
            shape((half, 8, width), F32),
        ),
        in_specs=[SMEM, pl.BlockSpec(memory_space=pltpu.HBM), VMEM, VMEM, VMEM],
        out_specs=(VMEM,) * 5,
        scratch_shapes=[pltpu.SemaphoreType.DMA((replicas,))],
        compiler_params=limit(20),
        cost_estimate=cost(24),
    )(parity, x_hbm, norm_gain, left_in[0].T, mine)
    power_t, kept, packed, send = pl.pallas_call(
        second_kernel,
        out_shape=(
            shape((rank, tokens), F32),
            shape((half, tokens, width), BF16),
            shape((8, width), F32),
            shape((half, height, width), BF16),
        ),
        in_specs=[SMEM] + [VMEM] * 7,
        out_specs=(VMEM,) * 4,
        scratch_shapes=[
            pltpu.VMEM((4, tokens, LANES), F32),
            pltpu.VMEM((half, tokens, width), F32),
            pltpu.VMEM((half, 8, width), F32),
            pltpu.VMEM((half, tokens, width), BF16),
            pltpu.VMEM((16, width), F32),
        ],
        compiler_params=limit(32),
    )(parity, x, norm_gain, left, rows, rebuilt, mine, theirs)
    other = lax.ppermute(send, "dp", others)
    keep = pl.pallas_call(
        third_kernel,
        out_shape=shape((half, rank, width), F32),
        in_specs=[VMEM] * 2,
        out_specs=VMEM,
        compiler_params=limit(12),
        cost_estimate=cost(12),
    )(power_t, kept)
    payload = pl.pallas_call(
        pair_kernel,
        out_shape=shape((half, height, width), BF16),
        in_specs=[VMEM] * 4,
        out_specs=VMEM,
        scratch_shapes=[pltpu.VMEM((16, width), F32)],
        compiler_params=limit(12),
    )(keep, packed, sums, other)
    terms = lax.all_to_all(payload, "dp", 0, 0, tiled=True, axis_index_groups=groups)

    factor = float(1.0 / (tokens * replicas) ** 0.5)
    gain_grad, bias_grad, moved = pl.pallas_call(
        lambda *refs: post_kernel(factor, *refs),
        out_shape=(shape((1, width), F32), shape((1, width), F32), shape((rank, width + tokens), BF16)),
        in_specs=[VMEM, VMEM],
        out_specs=(VMEM,) * 3,
        scratch_shapes=[pltpu.VMEM((24, LANES), F32)],
        compiler_params=limit(16),
    )(terms, power_t)
    sections = lax.axis_size("section")
    moved = lax.ppermute(moved, "section", [(i, i - 1) for i in range(1, sections)])
    left_out, right_out = pl.pallas_call(
        place_kernel,
        out_shape=(shape((rank, tokens), BF16), shape((rank, width), BF16)),
        in_specs=[VMEM],
        out_specs=(pl.BlockSpec(memory_space=pltpu.HBM),) * 2,
        scratch_shapes=[pltpu.SemaphoreType.DMA((2,))],
        compiler_params=limit(4),
    )(moved)
    return gain_grad, bias_grad, left_out.T[None], right_out.T[None]


def solution(mesh):
    placed = (
        P("section", "dp", None),
        P("section", None),
        P("section", "dp", None),
        P("section", "dp", None),
        P("section", "dp", None),
    )
    return jax.shard_map(
        on_device,
        mesh=mesh,
        in_specs=placed,
        out_specs=(
            P("section", "dp"),
            P("section", "dp"),
            P("section", "dp", None),
            P("section", "dp", None),
        ),
        check_vma=False,
    )
```

```python
import jax
import jax.numpy as jnp
from jax import lax
from jax.experimental import pallas as pl
from jax.experimental.pallas import tpu as pltpu
from jax.sharding import PartitionSpec as P

LANES = 128
GROUP = 16
UNROLL = 8
FETCH = 2
F32 = jnp.float32
BF16 = jnp.bfloat16
NT = (((1,), (1,)), ((), ()))
EXACT = dict(precision=lax.Precision.HIGHEST, preferred_element_type=F32)
VMEM = pl.BlockSpec(memory_space=pltpu.VMEM)
SMEM = pl.BlockSpec(memory_space=pltpu.SMEM)


def fold(value):
    return value[:8] + value[8:]


def gain_pass(j, k, left, factors, x, gain, rows, rebuilt, sums, plain=True, normal=True):
    tokens, width = rebuilt.shape[1:]
    rank = left.shape[1]
    chunks = range(width // LANES)
    columns = [pl.ds(pl.multiple_of(j * width + c * LANES, LANES), LANES) for c in chunks]
    gains = [jnp.broadcast_to(gain[:, columns[c]], (GROUP, LANES)) for c in chunks]
    products = [jnp.zeros((8, LANES), F32) for _ in chunks]
    bare = [jnp.zeros((8, LANES), F32) for _ in chunks]
    if plain:
        rebuilt[k] = jnp.dot(left, factors[k, :rank, :], preferred_element_type=F32)
    for r in range(0, tokens, GROUP):
        group = slice(r, r + GROUP)
        if normal:
            mean, inverse, second = rows[0, group], rows[1, group], rows[3, group]
        if plain:
            first = rows[2, group]
        for c in chunks:
            part = rebuilt[k, group, c * LANES : (c + 1) * LANES]
            scaled = part * gains[c]
            if plain:
                first = first + scaled
                bare[c] = bare[c] + fold(part)
            if normal:
                normed = (x[group, columns[c]].astype(F32) - mean) * inverse
                second = second + scaled * normed
                products[c] = products[c] + fold(part * normed)
        if plain:
            rows[2, group] = first
        if normal:
            rows[3, group] = second
    for c in chunks:
        lanes = slice(c * LANES, (c + 1) * LANES)
        if normal:
            sums[k, 0:1, lanes] = jnp.sum(products[c], axis=0, keepdims=True)
        if plain:
            sums[k, 1:2, lanes] = jnp.sum(bare[c], axis=0, keepdims=True)


def row_mean(total, features):
    return jnp.broadcast_to(jnp.sum(total, axis=1, keepdims=True) * (1.0 / features), total.shape)


def first_kernel(parity, x_hbm, gain, left_t, mine, x, left_out, rows, rebuilt, sums, arrived):
    half, _, width = mine.shape
    tokens, features = x.shape
    blocks = 2 * half
    chunks = range(width // LANES)

    def fetch(j):
        columns = pl.ds(pl.multiple_of(j * width, LANES), width)
        return pltpu.make_async_copy(x_hbm.at[:, columns], x.at[:, columns], arrived.at[j])

    @pl.loop(0, blocks)
    def _(j):
        fetch(j).start()

    left_out[...] = left_t[...].astype(F32).T.astype(BF16)
    left = left_out[...]
    rows[...] = jnp.zeros_like(rows)

    @pl.loop(0, half // UNROLL)
    def _(step):
        for k in [step * UNROLL + u for u in range(UNROLL)]:
            gain_pass(2 * k + parity[0], k, left, mine, x, gain, rows, rebuilt, sums, normal=False)

    for j in range(FETCH):
        fetch(j).wait()
    for r in range(0, tokens, GROUP):
        group = slice(r, r + GROUP)
        total = x[group, :LANES].astype(F32)
        for c in chunks[1:]:
            total = total + x[group, c * LANES : (c + 1) * LANES].astype(F32)
        rows[0, group] = row_mean(total, width)

    @pl.loop(0, blocks // FETCH)
    def _(step):
        @pl.when(step > 0)
        def _():
            for u in range(FETCH):
                fetch(step * FETCH + u).wait()

        for r in range(0, tokens, GROUP):
            group = slice(r, r + GROUP)
            base, total, squares = rows[0, group], rows[1, group], rows[3, group]
            for u in range(FETCH):
                for c in chunks:
                    start = (step * FETCH + u) * width + c * LANES
                    center = x[group, pl.ds(pl.multiple_of(start, LANES), LANES)].astype(F32) - base
                    total = total + center
                    squares = squares + center * center
            rows[1, group] = total
            rows[3, group] = squares

    shift = row_mean(rows[1], features)
    variance = jnp.maximum(row_mean(rows[3], features) - shift * shift, 0.0)
    rows[0] = rows[0] + shift
    rows[1] = lax.rsqrt(variance + 1e-05)
    rows[3] = jnp.zeros((tokens, LANES), F32)

    @pl.loop(0, half // UNROLL)
    def _(step):
        for k in [step * UNROLL + u for u in range(UNROLL)]:
            gain_pass(2 * k + parity[0], k, left, mine, x, gain, rows, rebuilt, sums, plain=False)


def second_kernel(
    parity, x, gain, left_ref, rows_in, rebuilt_mine, mine, theirs, power_t, kept, packed, send, rows, rebuilt, sums, moved, tail
):
    half, height, width = theirs.shape
    tokens, features = x.shape
    rank = left_ref.shape[1]
    chunks = range(width // LANES)
    left = left_ref[...]
    rows[...] = rows_in[...]

    def mixing(k, total):
        terms = []
        for side, factors in enumerate((mine, theirs)):
            start = (2 * k + (parity[0] ^ side)) * width
            scaled = factors[k, :rank, :] * gain[:, pl.ds(pl.multiple_of(start, LANES), width)].astype(BF16)
            terms.append(scaled)
        basis = jnp.concatenate([mine[k, rank:, :], theirs[k, rank:, :]], axis=0)
        both = lax.dot_general(basis, jnp.concatenate(terms, axis=0), NT, preferred_element_type=F32)
        return total + (both[:rank, :rank] + both[rank:, rank:])

    mixed = jnp.zeros((rank, rank), F32)
    for k in range(half):
        mixed = mixing(k, mixed)
        gain_pass(2 * k + (1 - parity[0]), k, left, theirs, x, gain, rows, rebuilt, sums)
    near = lax.dot_general(mixed, mixed, NT, **EXACT)
    row = lax.broadcasted_iota(jnp.int32, near.shape, 0)
    col = lax.broadcasted_iota(jnp.int32, near.shape, 1)
    level = jnp.sum(mixed * mixed) * (1e-06 / rank) + 1e-08
    lines = []
    steps = eliminate(near + jnp.where(row == col, level, 0.0), lines)

    first = row_mean(rows[2], features)
    second = row_mean(rows[3], features)
    rows[2] = rows[1] * rows[1] * second
    rows[3] = rows[0] * rows[2] - rows[1] * first

    def project(side, factors, source, target):
        def step(k, total):
            j = 2 * k + (parity[0] ^ side)
            columns = [pl.ds(pl.multiple_of(j * width + c * LANES, LANES), LANES) for c in chunks]
            gains = [jnp.broadcast_to(gain[:, columns[c]], (GROUP, LANES)) for c in chunks]
            groups = []
            for r in range(0, tokens, GROUP):
                group = slice(r, r + GROUP)
                inverse, slope, offset = rows[1, group], rows[2, group], rows[3, group]
                values = []
                for c in chunks:
                    lanes = slice(c * LANES, (c + 1) * LANES)
                    scaled = source[k, group, lanes] * gains[c]
                    value = scaled * inverse - x[group, columns[c]].astype(F32) * slope + offset
                    values.append(value.astype(BF16))
                    target[k, group, lanes] = values[-1]
                groups.append(jnp.concatenate(values, axis=1))
            block = jnp.concatenate(groups, axis=0)
            return total + lax.dot_general(block, factors[k, rank:, :], NT, preferred_element_type=F32)

        return step

    power = jnp.zeros((tokens, rank), F32)
    for k in range(half):
        power = project(0, mine, rebuilt_mine, kept)(k, power)
        next(steps)
    for k in range(half):
        power = project(1, theirs, rebuilt, moved)(k, power)
    basis_change = jnp.concatenate(lines, axis=0)
    power = lax.dot_general(basis_change, power, NT, **EXACT)
    power_t[...] = power
    pack(lax.dot_general(power, power, NT, **EXACT), packed)
    high = power.astype(BF16)
    split_gram(packed[0:4, :], tail)

    @pl.loop(0, half // UNROLL)
    def _(step):
        for k in [step * UNROLL + u for u in range(UNROLL)]:
            terms = jnp.dot(high, moved[k], preferred_element_type=F32)
            send[k, :rank, :] = terms.astype(BF16)
            split_sums(sums[k, 0:2, :], tail)
            send[k, rank:, :] = tail[...].astype(BF16)


def split(value, count):
    terms = []
    for _ in range(count):
        terms.append(value.astype(BF16).astype(F32))
        value = value - terms[-1]
    return terms


def split_sums(value, tail):
    for i, term in enumerate(split(value, 2)):
        tail[2 * i : 2 * i + 2, :] = term


def split_gram(value, tail):
    for i, term in enumerate(split(value, 3)):
        tail[4 + 4 * i : 8 + 4 * i, :] = term


def pack(gram, packed):
    size = gram.shape[0]
    half, quarter = size // 2, size // 4
    per = packed.shape[1] // LANES
    corner = gram[half:, half:]
    upper = jnp.concatenate([gram[:quarter], gram[quarter:half]], axis=1)
    lower = jnp.concatenate([corner[8 * i : 8 * i + 8] for i in range(half // 8)], axis=1)
    packed[...] = jnp.zeros_like(packed)
    for q in range(quarter + 8):
        line = upper[q : q + 1] if q < quarter else lower[q - quarter : q - quarter + 1]
        packed[q // per : q // per + 1, (q % per) * LANES : (q % per + 1) * LANES] = line


def unpack(packed, square):
    lines = square.shape[0]
    per = packed.shape[1] // LANES
    quarter = lines - 8
    half = 2 * quarter
    for q in range(lines):
        square[q : q + 1, :] = packed[q // per : q // per + 1, (q % per) * LANES : (q % per + 1) * LANES]
    upper = jnp.concatenate([square[:quarter, : 2 * half], square[:quarter, 2 * half :]], axis=0)
    corner = jnp.concatenate([square[quarter:, half * i : half * (i + 1)] for i in range(half // 8)], axis=0)
    return jnp.concatenate([upper, jnp.concatenate([upper[:, half:].T, corner], axis=1)], axis=0)


def third_kernel(power_t, kept, keep):
    high = power_t[...].astype(BF16)

    @pl.loop(0, keep.shape[0] // UNROLL)
    def _(step):
        for k in [step * UNROLL + u for u in range(UNROLL)]:
            keep[k] = jnp.dot(high, kept[k], preferred_element_type=F32)


def pair_kernel(keep, packed, sums, other, out, tail):
    half, rank, _ = keep.shape
    theirs = other[0, rank:, :].astype(F32)
    split_gram(packed[0:4, :] + (theirs[4:8] + (theirs[8:12] + theirs[12:16])), tail)

    @pl.loop(0, half // UNROLL)
    def _(step):
        for k in [step * UNROLL + u for u in range(UNROLL)]:
            out[k, :rank, :] = (keep[k] + other[k, :rank, :].astype(F32)).astype(BF16)
            theirs = other[k, rank:, :].astype(F32)
            split_sums(sums[k, 0:2, :] + (theirs[0:2] + theirs[2:4]), tail)
            out[k, rank:, :] = tail[...].astype(BF16)


def eliminate(gram, done):
    size = gram.shape[0]
    wide = 2 * size
    count = size // 8
    row = lax.broadcasted_iota(jnp.int32, (size, size), 0)
    col = lax.broadcasted_iota(jnp.int32, (size, size), 1)
    work = jnp.concatenate([gram, jnp.where(row == col, 1.0, 0.0).astype(F32)], axis=1)
    parts = [work[8 * i : 8 * i + 8] for i in range(count)]
    for b in range(count):
        below = range(b + 1, count)
        lines = [jnp.broadcast_to(parts[b][r : r + 1], (8, wide)) for r in range(8)]
        entry = {
            (i, j): jnp.broadcast_to(parts[b][i : i + 1, 8 * b + j : 8 * b + j + 1], (8, wide))
            for i in range(8)
            for j in range(i + 1)
        }
        factors = {(i, r): jnp.broadcast_to(parts[i][:, 8 * b + r : 8 * b + r + 1], (8, wide)) for i in below for r in range(8)}
        for r in range(8):
            scale = 1.0 / entry[r, r]
            for i in below:
                factors[i, r] = factors[i, r] * scale
            for q in range(r + 1, 8):
                ratio = entry[q, r] * scale
                for j in range(r + 1, q + 1):
                    entry[q, j] = entry[q, j] - ratio * entry[j, r]
                for i in below:
                    factors[i, q] = factors[i, q] - factors[i, r] * entry[q, r]
                lines[q] = lines[q] - ratio * lines[r]
        done += [(lines[r] * lax.rsqrt(entry[r, r]))[:1, size:] for r in range(8)]
        for i in below:
            terms = [factors[i, r] * lines[r] for r in range(8)]
            while len(terms) > 1:
                terms = [terms[t] + terms[t + 1] for t in range(0, len(terms), 2)]
            parts[i] = parts[i] - terms[0]
        yield


def inverse_factor(gram):
    done = []
    for _ in eliminate(gram, done):
        pass
    return jnp.concatenate(done, axis=0)


def post_kernel(factor, terms, power_t, gain_out, bias_out, moved, square):
    rank, tokens = power_t.shape
    width = terms.shape[2]
    total = terms[0].astype(F32)
    for j in range(1, terms.shape[0]):
        total = total + terms[j].astype(F32)
    extra = total[rank:]
    gain_out[...] = (extra[0:1] + extra[2:3]) * factor
    bias_out[...] = (extra[1:2] + extra[3:4]) * factor
    inverse = inverse_factor(unpack(extra[4:8] + (extra[8:12] + extra[12:16]), square))
    moved[:, :width] = jnp.dot(inverse, total[:rank], **EXACT).astype(BF16)
    moved[:, width:] = jnp.dot(inverse, power_t[...], **EXACT).astype(BF16)


def place_kernel(moved, gain, bias, left_out, right_out, gain_out, bias_out, sent):
    width = right_out.shape[1]
    pairs = ((moved.at[:, :width], right_out), (moved.at[:, width:], left_out), (gain, gain_out), (bias, bias_out))
    copies = [pltpu.make_async_copy(source, target, sent.at[i]) for i, (source, target) in enumerate(pairs)]
    for copy in copies:
        copy.start()
    for copy in copies:
        copy.wait()


def limit(mib):
    return pltpu.CompilerParams(vmem_limit_bytes=mib * 2**20)


def cost(mib):
    return pl.CostEstimate(flops=0, bytes_accessed=mib * 2**20, transcendentals=0)


def on_device(saved_input, norm_gain, left_in, right_in, basis):
    _, tokens, features = saved_input.shape
    width, rank = right_in.shape[1:]
    replicas = lax.axis_size("dp")
    half = replicas // 2
    height = rank + 16
    others = [(i, i ^ 1) for i in range(replicas)]
    groups = [[2 * k + c for k in range(half)] for c in range(2)]
    shape = jax.ShapeDtypeStruct

    x_hbm = pltpu.with_memory_space_constraint(saved_input[0], pltpu.HBM)
    own = jnp.concatenate([right_in[0].T, basis[0].T], axis=0)
    copies = jnp.broadcast_to(own[None], (half,) + own.shape)
    mine = lax.all_to_all(copies, "dp", 0, 0, tiled=True, axis_index_groups=groups)
    theirs = lax.ppermute(mine, "dp", others)
    parity = (lax.axis_index("dp") & 1).astype(jnp.int32).reshape(1)
    x, left, rows, rebuilt, sums = pl.pallas_call(
        first_kernel,
        out_shape=(
            shape((tokens, features), BF16),
            shape((tokens, rank), BF16),
            shape((4, tokens, LANES), F32),
            shape((half, tokens, width), F32),
            shape((half, 8, width), F32),
        ),
        in_specs=[SMEM, pl.BlockSpec(memory_space=pltpu.HBM), VMEM, VMEM, VMEM],
        out_specs=(VMEM,) * 5,
        scratch_shapes=[pltpu.SemaphoreType.DMA((replicas,))],
        compiler_params=limit(20),
        cost_estimate=cost(24),
    )(parity, x_hbm, norm_gain, left_in[0].T, mine)
    power_t, kept, packed, send = pl.pallas_call(
        second_kernel,
        out_shape=(
            shape((rank, tokens), F32),
            shape((half, tokens, width), BF16),
            shape((8, width), F32),
            shape((half, height, width), BF16),
        ),
        in_specs=[SMEM] + [VMEM] * 7,
        out_specs=(VMEM,) * 4,
        scratch_shapes=[
            pltpu.VMEM((4, tokens, LANES), F32),
            pltpu.VMEM((half, tokens, width), F32),
            pltpu.VMEM((half, 8, width), F32),
            pltpu.VMEM((half, tokens, width), BF16),
            pltpu.VMEM((16, width), F32),
        ],
        compiler_params=limit(32),
    )(parity, x, norm_gain, left, rows, rebuilt, mine, theirs)
    other = lax.ppermute(send, "dp", others)
    keep = pl.pallas_call(
        third_kernel,
        out_shape=shape((half, rank, width), F32),
        in_specs=[VMEM] * 2,
        out_specs=VMEM,
        compiler_params=limit(12),
        cost_estimate=cost(12),
    )(power_t, kept)
    payload = pl.pallas_call(
        pair_kernel,
        out_shape=shape((half, height, width), BF16),
        in_specs=[VMEM] * 4,
        out_specs=VMEM,
        scratch_shapes=[pltpu.VMEM((16, width), F32)],
        compiler_params=limit(12),
    )(keep, packed, sums, other)
    terms = lax.all_to_all(payload, "dp", 0, 0, tiled=True, axis_index_groups=groups)

    factor = float(1.0 / (tokens * replicas) ** 0.5)
    gain_sums, bias_sums, moved = pl.pallas_call(
        lambda *refs: post_kernel(factor, *refs),
        out_shape=(shape((1, width), F32), shape((1, width), F32), shape((rank, width + tokens), BF16)),
        in_specs=[VMEM, VMEM],
        out_specs=(VMEM,) * 3,
        scratch_shapes=[pltpu.VMEM((24, LANES), F32)],
        compiler_params=limit(16),
    )(terms, power_t)
    sections = lax.axis_size("section")
    moved = lax.ppermute(moved, "section", [(i, i - 1) for i in range(1, sections)])
    left_out, right_out, gain_grad, bias_grad = pl.pallas_call(
        place_kernel,
        out_shape=(shape((rank, tokens), BF16), shape((rank, width), BF16), shape((1, width), F32), shape((1, width), F32)),
        in_specs=[VMEM] * 3,
        out_specs=(pl.BlockSpec(memory_space=pltpu.HBM),) * 4,
        scratch_shapes=[pltpu.SemaphoreType.DMA((4,))],
        compiler_params=limit(4),
    )(moved, gain_sums, bias_sums)
    return gain_grad, bias_grad, left_out.T[None], right_out.T[None]


def solution(mesh):
    placed = (
        P("section", "dp", None),
        P("section", None),
        P("section", "dp", None),
        P("section", "dp", None),
        P("section", "dp", None),
    )
    return jax.shard_map(
        on_device,
        mesh=mesh,
        in_specs=placed,
        out_specs=(
            P("section", "dp"),
            P("section", "dp"),
            P("section", "dp", None),
            P("section", "dp", None),
        ),
        check_vma=False,
    )
```

```python
import jax
import jax.numpy as jnp
from jax import lax
from jax.experimental import pallas as pl
from jax.experimental.pallas import tpu as pltpu
from jax.sharding import PartitionSpec as P

LANES = 128
GROUP = 16
UNROLL = 8
FETCH = 2
F32 = jnp.float32
BF16 = jnp.bfloat16
NT = (((1,), (1,)), ((), ()))
EXACT = dict(precision=lax.Precision.HIGHEST, preferred_element_type=F32)
VMEM = pl.BlockSpec(memory_space=pltpu.VMEM)
SMEM = pl.BlockSpec(memory_space=pltpu.SMEM)


def fold(value):
    return value[:8] + value[8:]


def gain_pass(j, k, left, factors, x, gain, rows, rebuilt, sums, plain=True, normal=True):
    tokens, width = rebuilt.shape[1:]
    rank = left.shape[1]
    chunks = range(width // LANES)
    columns = [pl.ds(pl.multiple_of(j * width + c * LANES, LANES), LANES) for c in chunks]
    gains = [jnp.broadcast_to(gain[:, columns[c]], (GROUP, LANES)) for c in chunks]
    products = [jnp.zeros((8, LANES), F32) for _ in chunks]
    bare = [jnp.zeros((8, LANES), F32) for _ in chunks]
    if plain:
        rebuilt[k] = jnp.dot(left, factors[k, :rank, :], preferred_element_type=F32)
    for r in range(0, tokens, GROUP):
        group = slice(r, r + GROUP)
        if normal:
            mean, inverse, second = rows[0, group], rows[1, group], rows[3, group]
        if plain:
            first = rows[2, group]
        for c in chunks:
            part = rebuilt[k, group, c * LANES : (c + 1) * LANES]
            scaled = part * gains[c]
            if plain:
                first = first + scaled
                bare[c] = bare[c] + fold(part)
            if normal:
                normed = (x[group, columns[c]].astype(F32) - mean) * inverse
                second = second + scaled * normed
                products[c] = products[c] + fold(part * normed)
        if plain:
            rows[2, group] = first
        if normal:
            rows[3, group] = second
    for c in chunks:
        lanes = slice(c * LANES, (c + 1) * LANES)
        if normal:
            sums[k, 0:1, lanes] = jnp.sum(products[c], axis=0, keepdims=True)
        if plain:
            sums[k, 1:2, lanes] = jnp.sum(bare[c], axis=0, keepdims=True)


def row_mean(total, features):
    return jnp.broadcast_to(jnp.sum(total, axis=1, keepdims=True) * (1.0 / features), total.shape)


def copies_kernel(left_t, right_t, basis_t, copies, left, packed, arrived):
    rank = left_t.shape[0]
    own = copies.at[0]
    fetches = [
        pltpu.make_async_copy(left_t, left, arrived.at[0]),
        pltpu.make_async_copy(right_t, own.at[:rank, :], arrived.at[1]),
        pltpu.make_async_copy(basis_t, own.at[rank : 2 * rank, :], arrived.at[2]),
    ]
    for fetch in fetches:
        fetch.start()
    fetches[0].wait()
    pack(lax.dot_general(left[...], left[...], NT, preferred_element_type=F32), packed)
    copies[0, 2 * rank :, :] = jnp.concatenate(split(packed[0:4, :], 2), axis=0).astype(BF16)
    for fetch in fetches[1:]:
        fetch.wait()
    for k in range(1, copies.shape[0]):
        copies[k] = copies[0]


def first_kernel(parity, x_hbm, gain, left_t, mine, x, left_out, rows, rebuilt, sums, arrived):
    half, _, width = mine.shape
    tokens, features = x.shape
    blocks = 2 * half
    chunks = range(width // LANES)

    def fetch(j):
        columns = pl.ds(pl.multiple_of(j * width, LANES), width)
        return pltpu.make_async_copy(x_hbm.at[:, columns], x.at[:, columns], arrived.at[j])

    @pl.loop(0, blocks)
    def _(j):
        fetch(j).start()

    left_out[...] = left_t[...].astype(F32).T.astype(BF16)
    left = left_out[...]
    rows[...] = jnp.zeros_like(rows)

    @pl.loop(0, half // UNROLL)
    def _(step):
        for k in [step * UNROLL + u for u in range(UNROLL)]:
            gain_pass(2 * k + parity[0], k, left, mine, x, gain, rows, rebuilt, sums, normal=False)

    for j in range(FETCH):
        fetch(j).wait()
    for r in range(0, tokens, GROUP):
        group = slice(r, r + GROUP)
        total = x[group, :LANES].astype(F32)
        for c in chunks[1:]:
            total = total + x[group, c * LANES : (c + 1) * LANES].astype(F32)
        rows[0, group] = row_mean(total, width)

    @pl.loop(0, blocks // FETCH)
    def _(step):
        @pl.when(step > 0)
        def _():
            for u in range(FETCH):
                fetch(step * FETCH + u).wait()

        for r in range(0, tokens, GROUP):
            group = slice(r, r + GROUP)
            base, total, squares = rows[0, group], rows[1, group], rows[3, group]
            for u in range(FETCH):
                for c in chunks:
                    start = (step * FETCH + u) * width + c * LANES
                    center = x[group, pl.ds(pl.multiple_of(start, LANES), LANES)].astype(F32) - base
                    total = total + center
                    squares = squares + center * center
            rows[1, group] = total
            rows[3, group] = squares

    shift = row_mean(rows[1], features)
    variance = jnp.maximum(row_mean(rows[3], features) - shift * shift, 0.0)
    rows[0] = rows[0] + shift
    rows[1] = lax.rsqrt(variance + 1e-05)
    rows[3] = jnp.zeros((tokens, LANES), F32)

    @pl.loop(0, half // UNROLL)
    def _(step):
        for k in [step * UNROLL + u for u in range(UNROLL)]:
            gain_pass(2 * k + parity[0], k, left, mine, x, gain, rows, rebuilt, sums, plain=False)


def second_kernel(
    parity, x, gain, left_ref, rows_in, rebuilt_mine, mine, theirs, power_t, kept, packed, send, rows, rebuilt, sums, moved, tail, square
):
    half, height, width = theirs.shape
    tokens, features = x.shape
    rank = left_ref.shape[1]
    chunks = range(width // LANES)
    left = left_ref[...]
    rows[...] = rows_in[...]

    ones = jnp.ones((GROUP, width), BF16)

    def mixing(k, totals):
        terms = []
        for side, factors in enumerate((mine, theirs)):
            start = (2 * k + (parity[0] ^ side)) * width
            terms.append(factors[k, :rank, :] * gain[:, pl.ds(pl.multiple_of(start, LANES), width)].astype(BF16))
        basis = jnp.concatenate([mine[k, rank : 2 * rank, :], theirs[k, rank : 2 * rank, :], ones], axis=0)
        both = lax.dot_general(basis, jnp.concatenate(terms + [ones], axis=0), NT, preferred_element_type=F32)
        near, far = slice(0, rank), slice(rank, 2 * rank)
        last = slice(2 * rank, 2 * rank + 1)
        spread = [factors[k, 2 * rank :, :].astype(F32) for factors in (mine, theirs)]
        values = (
            both[near, near] + both[far, far],
            both[near, last] + both[far, last],
            both[last, near] + both[last, far],
            spread[0] + spread[1],
        )
        return tuple(total + value for total, value in zip(totals, values))

    totals = (jnp.zeros((rank, rank), F32), jnp.zeros((rank, 1), F32), jnp.zeros((1, rank), F32), jnp.zeros((8, width), F32))
    for k in range(half):
        totals = mixing(k, totals)
        gain_pass(2 * k + (1 - parity[0]), k, left, theirs, x, gain, rows, rebuilt, sums)
    mixed = totals[0] - totals[1] * (totals[2] * (1.0 / features))
    spread = unpack(totals[3][0:4] + totals[3][4:8], square) * (1.0 / (2 * half * tokens))
    near = lax.dot_general(jnp.dot(mixed, spread, **EXACT), mixed, NT, **EXACT)
    row = lax.broadcasted_iota(jnp.int32, near.shape, 0)
    col = lax.broadcasted_iota(jnp.int32, near.shape, 1)
    level = jnp.sum(jnp.where(row == col, near, 0.0)) * 1e-05 + 1e-08
    lines = []
    steps = eliminate(near + jnp.where(row == col, level, 0.0), lines, 0.25 * level)

    first = row_mean(rows[2], features)
    second = row_mean(rows[3], features)
    rows[2] = rows[1] * rows[1] * second
    rows[3] = rows[0] * rows[2] - rows[1] * first

    def project(side, factors, source, target):
        def step(k, total):
            j = 2 * k + (parity[0] ^ side)
            columns = [pl.ds(pl.multiple_of(j * width + c * LANES, LANES), LANES) for c in chunks]
            gains = [jnp.broadcast_to(gain[:, columns[c]], (GROUP, LANES)) for c in chunks]
            groups = []
            for r in range(0, tokens, GROUP):
                group = slice(r, r + GROUP)
                inverse, slope, offset = rows[1, group], rows[2, group], rows[3, group]
                values = []
                for c in chunks:
                    lanes = slice(c * LANES, (c + 1) * LANES)
                    scaled = source[k, group, lanes] * gains[c]
                    value = scaled * inverse - x[group, columns[c]].astype(F32) * slope + offset
                    values.append(value.astype(BF16))
                    target[k, group, lanes] = values[-1]
                groups.append(jnp.concatenate(values, axis=1))
            block = jnp.concatenate(groups, axis=0)
            return total + lax.dot_general(block, factors[k, rank : 2 * rank, :], NT, preferred_element_type=F32)

        return step

    power = jnp.zeros((tokens, rank), F32)
    for k in range(half):
        power = project(0, mine, rebuilt_mine, kept)(k, power)
        next(steps)
    for k in range(half):
        power = project(1, theirs, rebuilt, moved)(k, power)
    basis_change = jnp.concatenate(lines, axis=0)
    power = lax.dot_general(basis_change, power, NT, **EXACT)
    power_t[...] = power
    pack(lax.dot_general(power, power, NT, **EXACT), packed)
    high = power.astype(BF16)
    split_gram(packed[0:4, :], tail)

    @pl.loop(0, half // UNROLL)
    def _(step):
        for k in [step * UNROLL + u for u in range(UNROLL)]:
            terms = jnp.dot(high, moved[k], preferred_element_type=F32)
            send[k, :rank, :] = terms.astype(BF16)
            split_sums(sums[k, 0:2, :], tail)
            send[k, rank:, :] = tail[...].astype(BF16)


def split(value, count):
    terms = []
    for _ in range(count):
        terms.append(value.astype(BF16).astype(F32))
        value = value - terms[-1]
    return terms


def split_sums(value, tail):
    for i, term in enumerate(split(value, 2)):
        tail[2 * i : 2 * i + 2, :] = term


def split_gram(value, tail):
    for i, term in enumerate(split(value, 3)):
        tail[4 + 4 * i : 8 + 4 * i, :] = term


def pack(gram, packed):
    size = gram.shape[0]
    half, quarter = size // 2, size // 4
    per = packed.shape[1] // LANES
    corner = gram[half:, half:]
    upper = jnp.concatenate([gram[:quarter], gram[quarter:half]], axis=1)
    lower = jnp.concatenate([corner[8 * i : 8 * i + 8] for i in range(half // 8)], axis=1)
    packed[...] = jnp.zeros_like(packed)
    for q in range(quarter + 8):
        line = upper[q : q + 1] if q < quarter else lower[q - quarter : q - quarter + 1]
        packed[q // per : q // per + 1, (q % per) * LANES : (q % per + 1) * LANES] = line


def unpack(packed, square):
    lines = square.shape[0]
    per = packed.shape[1] // LANES
    quarter = lines - 8
    half = 2 * quarter
    for q in range(lines):
        square[q : q + 1, :] = packed[q // per : q // per + 1, (q % per) * LANES : (q % per + 1) * LANES]
    upper = jnp.concatenate([square[:quarter, : 2 * half], square[:quarter, 2 * half :]], axis=0)
    corner = jnp.concatenate([square[quarter:, half * i : half * (i + 1)] for i in range(half // 8)], axis=0)
    return jnp.concatenate([upper, jnp.concatenate([upper[:, half:].T, corner], axis=1)], axis=0)


def third_kernel(power_t, kept, keep):
    high = power_t[...].astype(BF16)

    @pl.loop(0, keep.shape[0] // UNROLL)
    def _(step):
        for k in [step * UNROLL + u for u in range(UNROLL)]:
            keep[k] = jnp.dot(high, kept[k], preferred_element_type=F32)


def pair_kernel(keep, packed, sums, other, out, tail):
    half, rank, _ = keep.shape
    theirs = other[0, rank:, :].astype(F32)
    split_gram(packed[0:4, :] + (theirs[4:8] + (theirs[8:12] + theirs[12:16])), tail)

    @pl.loop(0, half // UNROLL)
    def _(step):
        for k in [step * UNROLL + u for u in range(UNROLL)]:
            out[k, :rank, :] = (keep[k] + other[k, :rank, :].astype(F32)).astype(BF16)
            theirs = other[k, rank:, :].astype(F32)
            split_sums(sums[k, 0:2, :] + (theirs[0:2] + theirs[2:4]), tail)
            out[k, rank:, :] = tail[...].astype(BF16)


def eliminate(gram, done, floor=None):
    size = gram.shape[0]
    wide = 2 * size
    count = size // 8
    row = lax.broadcasted_iota(jnp.int32, (size, size), 0)
    col = lax.broadcasted_iota(jnp.int32, (size, size), 1)
    work = jnp.concatenate([gram, jnp.where(row == col, 1.0, 0.0).astype(F32)], axis=1)
    parts = [work[8 * i : 8 * i + 8] for i in range(count)]
    for b in range(count):
        below = range(b + 1, count)
        lines = [jnp.broadcast_to(parts[b][r : r + 1], (8, wide)) for r in range(8)]
        entry = {
            (i, j): jnp.broadcast_to(parts[b][i : i + 1, 8 * b + j : 8 * b + j + 1], (8, wide))
            for i in range(8)
            for j in range(i + 1)
        }
        factors = {(i, r): jnp.broadcast_to(parts[i][:, 8 * b + r : 8 * b + r + 1], (8, wide)) for i in below for r in range(8)}
        for r in range(8):
            if floor is not None:
                entry[r, r] = jnp.maximum(entry[r, r], floor)
            scale = 1.0 / entry[r, r]
            for i in below:
                factors[i, r] = factors[i, r] * scale
            for q in range(r + 1, 8):
                ratio = entry[q, r] * scale
                for j in range(r + 1, q + 1):
                    entry[q, j] = entry[q, j] - ratio * entry[j, r]
                for i in below:
                    factors[i, q] = factors[i, q] - factors[i, r] * entry[q, r]
                lines[q] = lines[q] - ratio * lines[r]
        done += [(lines[r] * lax.rsqrt(entry[r, r]))[:1, size:] for r in range(8)]
        for i in below:
            terms = [factors[i, r] * lines[r] for r in range(8)]
            while len(terms) > 1:
                terms = [terms[t] + terms[t + 1] for t in range(0, len(terms), 2)]
            parts[i] = parts[i] - terms[0]
        yield


def inverse_factor(gram):
    done = []
    for _ in eliminate(gram, done):
        pass
    return jnp.concatenate(done, axis=0)


def post_kernel(factor, terms, power_t, gain_out, bias_out, moved, square):
    rank, tokens = power_t.shape
    width = terms.shape[2]
    total = terms[0].astype(F32)
    for j in range(1, terms.shape[0]):
        total = total + terms[j].astype(F32)
    extra = total[rank:]
    gain_out[...] = (extra[0:1] + extra[2:3]) * factor
    bias_out[...] = (extra[1:2] + extra[3:4]) * factor
    inverse = inverse_factor(unpack(extra[4:8] + (extra[8:12] + extra[12:16]), square))
    moved[:, :width] = jnp.dot(inverse, total[:rank], **EXACT).astype(BF16)
    moved[:, width:] = jnp.dot(inverse, power_t[...], **EXACT).astype(BF16)


def place_kernel(moved, gain, bias, left_out, right_out, gain_out, bias_out, sent):
    width = right_out.shape[1]
    pairs = ((moved.at[:, :width], right_out), (moved.at[:, width:], left_out), (gain, gain_out), (bias, bias_out))
    copies = [pltpu.make_async_copy(source, target, sent.at[i]) for i, (source, target) in enumerate(pairs)]
    for copy in copies:
        copy.start()
    for copy in copies:
        copy.wait()


def limit(mib):
    return pltpu.CompilerParams(vmem_limit_bytes=mib * 2**20)


def cost(mib):
    return pl.CostEstimate(flops=0, bytes_accessed=mib * 2**20, transcendentals=0)


def on_device(saved_input, norm_gain, left_in, right_in, basis):
    _, tokens, features = saved_input.shape
    width, rank = right_in.shape[1:]
    replicas = lax.axis_size("dp")
    half = replicas // 2
    height = rank + 16
    others = [(i, i ^ 1) for i in range(replicas)]
    groups = [[2 * k + c for k in range(half)] for c in range(2)]
    shape = jax.ShapeDtypeStruct

    x_hbm = pltpu.with_memory_space_constraint(saved_input[0], pltpu.HBM)
    own = [pltpu.with_memory_space_constraint(factor[0].T, pltpu.HBM) for factor in (left_in, right_in, basis)]
    copies = pl.pallas_call(
        copies_kernel,
        out_shape=shape((half, 2 * rank + 8, width), BF16),
        in_specs=[pl.BlockSpec(memory_space=pltpu.HBM)] * 3,
        out_specs=VMEM,
        scratch_shapes=[pltpu.VMEM((rank, tokens), BF16), pltpu.VMEM((8, width), F32), pltpu.SemaphoreType.DMA((3,))],
        compiler_params=limit(4),
    )(*own)
    mine = lax.all_to_all(copies, "dp", 0, 0, tiled=True, axis_index_groups=groups)
    theirs = lax.ppermute(mine, "dp", others)
    parity = (lax.axis_index("dp") & 1).astype(jnp.int32).reshape(1)
    x, left, rows, rebuilt, sums = pl.pallas_call(
        first_kernel,
        out_shape=(
            shape((tokens, features), BF16),
            shape((tokens, rank), BF16),
            shape((4, tokens, LANES), F32),
            shape((half, tokens, width), F32),
            shape((half, 8, width), F32),
        ),
        in_specs=[SMEM, pl.BlockSpec(memory_space=pltpu.HBM), VMEM, VMEM, VMEM],
        out_specs=(VMEM,) * 5,
        scratch_shapes=[pltpu.SemaphoreType.DMA((replicas,))],
        compiler_params=limit(20),
        cost_estimate=cost(24),
    )(parity, x_hbm, norm_gain, left_in[0].T, mine)
    power_t, kept, packed, send = pl.pallas_call(
        second_kernel,
        out_shape=(
            shape((rank, tokens), F32),
            shape((half, tokens, width), BF16),
            shape((8, width), F32),
            shape((half, height, width), BF16),
        ),
        in_specs=[SMEM] + [VMEM] * 7,
        out_specs=(VMEM,) * 4,
        scratch_shapes=[
            pltpu.VMEM((4, tokens, LANES), F32),
            pltpu.VMEM((half, tokens, width), F32),
            pltpu.VMEM((half, 8, width), F32),
            pltpu.VMEM((half, tokens, width), BF16),
            pltpu.VMEM((16, width), F32),
            pltpu.VMEM((24, LANES), F32),
        ],
        compiler_params=limit(32),
    )(parity, x, norm_gain, left, rows, rebuilt, mine, theirs)
    other = lax.ppermute(send, "dp", others)
    keep = pl.pallas_call(
        third_kernel,
        out_shape=shape((half, rank, width), F32),
        in_specs=[VMEM] * 2,
        out_specs=VMEM,
        compiler_params=limit(12),
        cost_estimate=cost(12),
    )(power_t, kept)
    payload = pl.pallas_call(
        pair_kernel,
        out_shape=shape((half, height, width), BF16),
        in_specs=[VMEM] * 4,
        out_specs=VMEM,
        scratch_shapes=[pltpu.VMEM((16, width), F32)],
        compiler_params=limit(12),
    )(keep, packed, sums, other)
    terms = lax.all_to_all(payload, "dp", 0, 0, tiled=True, axis_index_groups=groups)

    factor = float(1.0 / (tokens * replicas) ** 0.5)
    gain_sums, bias_sums, moved = pl.pallas_call(
        lambda *refs: post_kernel(factor, *refs),
        out_shape=(shape((1, width), F32), shape((1, width), F32), shape((rank, width + tokens), BF16)),
        in_specs=[VMEM, VMEM],
        out_specs=(VMEM,) * 3,
        scratch_shapes=[pltpu.VMEM((24, LANES), F32)],
        compiler_params=limit(16),
    )(terms, power_t)
    sections = lax.axis_size("section")
    moved = lax.ppermute(moved, "section", [(i, i - 1) for i in range(1, sections)])
    left_out, right_out, gain_grad, bias_grad = pl.pallas_call(
        place_kernel,
        out_shape=(shape((rank, tokens), BF16), shape((rank, width), BF16), shape((1, width), F32), shape((1, width), F32)),
        in_specs=[VMEM] * 3,
        out_specs=(pl.BlockSpec(memory_space=pltpu.HBM),) * 4,
        scratch_shapes=[pltpu.SemaphoreType.DMA((4,))],
        compiler_params=limit(4),
    )(moved, gain_sums, bias_sums)
    return gain_grad, bias_grad, left_out.T[None], right_out.T[None]


def solution(mesh):
    placed = (
        P("section", "dp", None),
        P("section", None),
        P("section", "dp", None),
        P("section", "dp", None),
        P("section", "dp", None),
    )
    return jax.shard_map(
        on_device,
        mesh=mesh,
        in_specs=placed,
        out_specs=(
            P("section", "dp"),
            P("section", "dp"),
            P("section", "dp", None),
            P("section", "dp", None),
        ),
        check_vma=False,
    )
```

```python
import jax
import jax.numpy as jnp
from jax import lax
from jax.experimental import pallas as pl
from jax.experimental.pallas import tpu as pltpu
from jax.sharding import PartitionSpec as P

LANES = 128
GROUP = 16
UNROLL = 8
FETCH = 2
F32 = jnp.float32
BF16 = jnp.bfloat16
NT = (((1,), (1,)), ((), ()))
EXACT = dict(precision=lax.Precision.HIGHEST, preferred_element_type=F32)
VMEM = pl.BlockSpec(memory_space=pltpu.VMEM)
SMEM = pl.BlockSpec(memory_space=pltpu.SMEM)


def fold(value):
    return value[:8] + value[8:]


def gain_pass(j, k, left, factors, x, gain, rows, rebuilt, sums, plain=True, normal=True):
    tokens, width = rebuilt.shape[1:]
    rank = left.shape[1]
    chunks = range(width // LANES)
    columns = [pl.ds(pl.multiple_of(j * width + c * LANES, LANES), LANES) for c in chunks]
    gains = [jnp.broadcast_to(gain[:, columns[c]], (GROUP, LANES)) for c in chunks]
    products = [jnp.zeros((8, LANES), F32) for _ in chunks]
    bare = [jnp.zeros((8, LANES), F32) for _ in chunks]
    if plain:
        rebuilt[k] = jnp.dot(left, factors[k, :rank, :], preferred_element_type=F32)
    for r in range(0, tokens, GROUP):
        group = slice(r, r + GROUP)
        if normal:
            mean, inverse, second = rows[0, group], rows[1, group], rows[3, group]
        if plain:
            first = rows[2, group]
        for c in chunks:
            part = rebuilt[k, group, c * LANES : (c + 1) * LANES]
            scaled = part * gains[c]
            if plain:
                first = first + scaled
                bare[c] = bare[c] + fold(part)
            if normal:
                normed = (x[group, columns[c]].astype(F32) - mean) * inverse
                second = second + scaled * normed
                products[c] = products[c] + fold(part * normed)
                rebuilt[k, group, c * LANES : (c + 1) * LANES] = scaled
        if plain:
            rows[2, group] = first
        if normal:
            rows[3, group] = second
    for c in chunks:
        lanes = slice(c * LANES, (c + 1) * LANES)
        if normal:
            sums[k, 0:1, lanes] = jnp.sum(products[c], axis=0, keepdims=True)
        if plain:
            sums[k, 1:2, lanes] = jnp.sum(bare[c], axis=0, keepdims=True)


def row_mean(total, features):
    return jnp.broadcast_to(jnp.sum(total, axis=1, keepdims=True) * (1.0 / features), total.shape)


def copies_kernel(left_t, right_t, basis_t, copies, left, packed, arrived):
    rank = left_t.shape[0]
    own = copies.at[0]
    fetches = [
        pltpu.make_async_copy(left_t, left, arrived.at[0]),
        pltpu.make_async_copy(right_t, own.at[:rank, :], arrived.at[1]),
        pltpu.make_async_copy(basis_t, own.at[rank : 2 * rank, :], arrived.at[2]),
    ]
    for fetch in fetches:
        fetch.start()
    fetches[0].wait()
    pack(lax.dot_general(left[...], left[...], NT, preferred_element_type=F32), packed)
    copies[0, 2 * rank :, :] = jnp.concatenate(split(packed[0:4, :], 2), axis=0).astype(BF16)
    for fetch in fetches[1:]:
        fetch.wait()
    for k in range(1, copies.shape[0]):
        copies[k] = copies[0]


def first_kernel(parity, x_hbm, gain, left_t, mine, x, left_out, rows, rebuilt, sums, arrived):
    half, _, width = mine.shape
    tokens, features = x.shape
    blocks = 2 * half
    chunks = range(width // LANES)

    def fetch(j):
        columns = pl.ds(pl.multiple_of(j * width, LANES), width)
        return pltpu.make_async_copy(x_hbm.at[:, columns], x.at[:, columns], arrived.at[j])

    @pl.loop(0, blocks)
    def _(j):
        fetch(j).start()

    left_out[...] = left_t[...].astype(F32).T.astype(BF16)
    left = left_out[...]
    rows[...] = jnp.zeros_like(rows)

    @pl.loop(0, half // UNROLL)
    def _(step):
        for k in [step * UNROLL + u for u in range(UNROLL)]:
            gain_pass(2 * k + parity[0], k, left, mine, x, gain, rows, rebuilt, sums, normal=False)

    for j in range(FETCH):
        fetch(j).wait()
    for r in range(0, tokens, GROUP):
        group = slice(r, r + GROUP)
        total = x[group, :LANES].astype(F32)
        for c in chunks[1:]:
            total = total + x[group, c * LANES : (c + 1) * LANES].astype(F32)
        rows[0, group] = row_mean(total, width)

    @pl.loop(0, blocks // FETCH)
    def _(step):
        @pl.when(step > 0)
        def _():
            for u in range(FETCH):
                fetch(step * FETCH + u).wait()

        for r in range(0, tokens, GROUP):
            group = slice(r, r + GROUP)
            base, total, squares = rows[0, group], rows[1, group], rows[3, group]
            for u in range(FETCH):
                for c in chunks:
                    start = (step * FETCH + u) * width + c * LANES
                    center = x[group, pl.ds(pl.multiple_of(start, LANES), LANES)].astype(F32) - base
                    total = total + center
                    squares = squares + center * center
            rows[1, group] = total
            rows[3, group] = squares

    shift = row_mean(rows[1], features)
    variance = jnp.maximum(row_mean(rows[3], features) - shift * shift, 0.0)
    rows[0] = rows[0] + shift
    rows[1] = lax.rsqrt(variance + 1e-05)
    rows[3] = jnp.zeros((tokens, LANES), F32)

    @pl.loop(0, half // UNROLL)
    def _(step):
        for k in [step * UNROLL + u for u in range(UNROLL)]:
            gain_pass(2 * k + parity[0], k, left, mine, x, gain, rows, rebuilt, sums, plain=False)


def second_kernel(
    parity, x, gain, left_ref, rows_in, rebuilt_mine, mine, theirs, power_t, kept, packed, send, rows, rebuilt, sums, moved, tail, square
):
    half, height, width = theirs.shape
    tokens, features = x.shape
    rank = left_ref.shape[1]
    chunks = range(width // LANES)
    left = left_ref[...]
    rows[...] = rows_in[...]

    ones = jnp.ones((GROUP, width), BF16)

    def mixing(k, totals):
        terms = []
        for side, factors in enumerate((mine, theirs)):
            start = (2 * k + (parity[0] ^ side)) * width
            terms.append(factors[k, :rank, :] * gain[:, pl.ds(pl.multiple_of(start, LANES), width)].astype(BF16))
        basis = jnp.concatenate([mine[k, rank : 2 * rank, :], theirs[k, rank : 2 * rank, :], ones], axis=0)
        both = lax.dot_general(basis, jnp.concatenate(terms + [ones], axis=0), NT, preferred_element_type=F32)
        near, far = slice(0, rank), slice(rank, 2 * rank)
        last = slice(2 * rank, 2 * rank + 1)
        spread = [factors[k, 2 * rank :, :].astype(F32) for factors in (mine, theirs)]
        values = (
            both[near, near] + both[far, far],
            both[near, last] + both[far, last],
            both[last, near] + both[last, far],
            spread[0] + spread[1],
        )
        return tuple(total + value for total, value in zip(totals, values))

    totals = (jnp.zeros((rank, rank), F32), jnp.zeros((rank, 1), F32), jnp.zeros((1, rank), F32), jnp.zeros((8, width), F32))
    for k in range(half):
        totals = mixing(k, totals)
        gain_pass(2 * k + (1 - parity[0]), k, left, theirs, x, gain, rows, rebuilt, sums)
    mixed = totals[0] - totals[1] * (totals[2] * (1.0 / features))
    spread = unpack(totals[3][0:4] + totals[3][4:8], square) * (1.0 / (2 * half * tokens))
    near = lax.dot_general(jnp.dot(mixed, spread, **EXACT), mixed, NT, **EXACT)
    row = lax.broadcasted_iota(jnp.int32, near.shape, 0)
    col = lax.broadcasted_iota(jnp.int32, near.shape, 1)
    level = jnp.sum(jnp.where(row == col, near, 0.0)) * 1e-05 + 1e-08
    lines = []
    steps = eliminate(near + jnp.where(row == col, level, 0.0), lines, 0.25 * level)

    first = row_mean(rows[2], features)
    second = row_mean(rows[3], features)
    rows[2] = rows[1] * rows[1] * second
    rows[3] = rows[0] * rows[2] - rows[1] * first

    def project(side, factors, source, target):
        def step(k, total):
            j = 2 * k + (parity[0] ^ side)
            columns = [pl.ds(pl.multiple_of(j * width + c * LANES, LANES), LANES) for c in chunks]
            groups = []
            for r in range(0, tokens, GROUP):
                group = slice(r, r + GROUP)
                inverse, slope, offset = rows[1, group], rows[2, group], rows[3, group]
                values = []
                for c in chunks:
                    lanes = slice(c * LANES, (c + 1) * LANES)
                    value = source[k, group, lanes] * inverse - x[group, columns[c]].astype(F32) * slope + offset
                    values.append(value.astype(BF16))
                    target[k, group, lanes] = values[-1]
                groups.append(jnp.concatenate(values, axis=1))
            block = jnp.concatenate(groups, axis=0)
            return total + lax.dot_general(block, factors[k, rank : 2 * rank, :], NT, preferred_element_type=F32)

        return step

    power = jnp.zeros((tokens, rank), F32)
    for k in range(half):
        power = project(0, mine, rebuilt_mine, kept)(k, power)
        next(steps)
    for k in range(half):
        power = project(1, theirs, rebuilt, moved)(k, power)
    basis_change = jnp.concatenate(lines, axis=0)
    power = lax.dot_general(basis_change, power, NT, **EXACT)
    power_t[...] = power
    pack(lax.dot_general(power, power, NT, **EXACT), packed)
    high = power.astype(BF16)
    split_gram(packed[0:4, :], tail)

    @pl.loop(0, half // UNROLL)
    def _(step):
        for k in [step * UNROLL + u for u in range(UNROLL)]:
            terms = jnp.dot(high, moved[k], preferred_element_type=F32)
            send[k, :rank, :] = terms.astype(BF16)
            split_sums(sums[k, 0:2, :], tail)
            send[k, rank:, :] = tail[...].astype(BF16)


def split(value, count):
    terms = []
    for _ in range(count):
        terms.append(value.astype(BF16).astype(F32))
        value = value - terms[-1]
    return terms


def split_sums(value, tail):
    for i, term in enumerate(split(value, 2)):
        tail[2 * i : 2 * i + 2, :] = term


def split_gram(value, tail):
    for i, term in enumerate(split(value, 3)):
        tail[4 + 4 * i : 8 + 4 * i, :] = term


def pack(gram, packed):
    size = gram.shape[0]
    half, quarter = size // 2, size // 4
    per = packed.shape[1] // LANES
    corner = gram[half:, half:]
    upper = jnp.concatenate([gram[:quarter], gram[quarter:half]], axis=1)
    lower = jnp.concatenate([corner[8 * i : 8 * i + 8] for i in range(half // 8)], axis=1)
    packed[...] = jnp.zeros_like(packed)
    for q in range(quarter + 8):
        line = upper[q : q + 1] if q < quarter else lower[q - quarter : q - quarter + 1]
        packed[q // per : q // per + 1, (q % per) * LANES : (q % per + 1) * LANES] = line


def unpack(packed, square):
    lines = square.shape[0]
    per = packed.shape[1] // LANES
    quarter = lines - 8
    half = 2 * quarter
    for q in range(lines):
        square[q : q + 1, :] = packed[q // per : q // per + 1, (q % per) * LANES : (q % per + 1) * LANES]
    upper = jnp.concatenate([square[:quarter, : 2 * half], square[:quarter, 2 * half :]], axis=0)
    corner = jnp.concatenate([square[quarter:, half * i : half * (i + 1)] for i in range(half // 8)], axis=0)
    return jnp.concatenate([upper, jnp.concatenate([upper[:, half:].T, corner], axis=1)], axis=0)


def third_kernel(power_t, kept, keep):
    high = power_t[...].astype(BF16)

    @pl.loop(0, keep.shape[0] // UNROLL)
    def _(step):
        for k in [step * UNROLL + u for u in range(UNROLL)]:
            keep[k] = jnp.dot(high, kept[k], preferred_element_type=F32)


def pair_kernel(keep, packed, sums, other, out, tail):
    half, rank, _ = keep.shape
    theirs = other[0, rank:, :].astype(F32)
    split_gram(packed[0:4, :] + (theirs[4:8] + (theirs[8:12] + theirs[12:16])), tail)

    @pl.loop(0, half // UNROLL)
    def _(step):
        for k in [step * UNROLL + u for u in range(UNROLL)]:
            out[k, :rank, :] = (keep[k] + other[k, :rank, :].astype(F32)).astype(BF16)
            theirs = other[k, rank:, :].astype(F32)
            split_sums(sums[k, 0:2, :] + (theirs[0:2] + theirs[2:4]), tail)
            out[k, rank:, :] = tail[...].astype(BF16)


def eliminate(gram, done, floor=None):
    size = gram.shape[0]
    wide = 2 * size
    count = size // 8
    row = lax.broadcasted_iota(jnp.int32, (size, size), 0)
    col = lax.broadcasted_iota(jnp.int32, (size, size), 1)
    work = jnp.concatenate([gram, jnp.where(row == col, 1.0, 0.0).astype(F32)], axis=1)
    parts = [work[8 * i : 8 * i + 8] for i in range(count)]
    for b in range(count):
        below = range(b + 1, count)
        lines = [jnp.broadcast_to(parts[b][r : r + 1], (8, wide)) for r in range(8)]
        entry = {
            (i, j): jnp.broadcast_to(parts[b][i : i + 1, 8 * b + j : 8 * b + j + 1], (8, wide))
            for i in range(8)
            for j in range(i + 1)
        }
        factors = {(i, r): jnp.broadcast_to(parts[i][:, 8 * b + r : 8 * b + r + 1], (8, wide)) for i in below for r in range(8)}
        for r in range(8):
            if floor is not None:
                entry[r, r] = jnp.maximum(entry[r, r], floor)
            scale = 1.0 / entry[r, r]
            for i in below:
                factors[i, r] = factors[i, r] * scale
            for q in range(r + 1, 8):
                ratio = entry[q, r] * scale
                for j in range(r + 1, q + 1):
                    entry[q, j] = entry[q, j] - ratio * entry[j, r]
                for i in below:
                    factors[i, q] = factors[i, q] - factors[i, r] * entry[q, r]
                lines[q] = lines[q] - ratio * lines[r]
        done += [(lines[r] * lax.rsqrt(entry[r, r]))[:1, size:] for r in range(8)]
        for i in below:
            terms = [factors[i, r] * lines[r] for r in range(8)]
            while len(terms) > 1:
                terms = [terms[t] + terms[t + 1] for t in range(0, len(terms), 2)]
            parts[i] = parts[i] - terms[0]
        yield


def inverse_factor(gram):
    done = []
    for _ in eliminate(gram, done):
        pass
    return jnp.concatenate(done, axis=0)


def post_kernel(factor, terms, power_t, gain_out, bias_out, moved, square):
    rank, tokens = power_t.shape
    width = terms.shape[2]
    total = terms[0].astype(F32)
    for j in range(1, terms.shape[0]):
        total = total + terms[j].astype(F32)
    extra = total[rank:]
    gain_out[...] = (extra[0:1] + extra[2:3]) * factor
    bias_out[...] = (extra[1:2] + extra[3:4]) * factor
    inverse = inverse_factor(unpack(extra[4:8] + (extra[8:12] + extra[12:16]), square))
    moved[:, :width] = jnp.dot(inverse, total[:rank], **EXACT).astype(BF16)
    moved[:, width:] = jnp.dot(inverse, power_t[...], **EXACT).astype(BF16)


def place_kernel(moved, gain, bias, left_out, right_out, gain_out, bias_out, sent):
    width = right_out.shape[1]
    pairs = ((moved.at[:, :width], right_out), (moved.at[:, width:], left_out), (gain, gain_out), (bias, bias_out))
    copies = [pltpu.make_async_copy(source, target, sent.at[i]) for i, (source, target) in enumerate(pairs)]
    for copy in copies:
        copy.start()
    for copy in copies:
        copy.wait()


def limit(mib):
    return pltpu.CompilerParams(vmem_limit_bytes=mib * 2**20)


def cost(mib):
    return pl.CostEstimate(flops=0, bytes_accessed=mib * 2**20, transcendentals=0)


def on_device(saved_input, norm_gain, left_in, right_in, basis):
    _, tokens, features = saved_input.shape
    width, rank = right_in.shape[1:]
    replicas = lax.axis_size("dp")
    half = replicas // 2
    height = rank + 16
    others = [(i, i ^ 1) for i in range(replicas)]
    groups = [[2 * k + c for k in range(half)] for c in range(2)]
    shape = jax.ShapeDtypeStruct

    x_hbm = pltpu.with_memory_space_constraint(saved_input[0], pltpu.HBM)
    own = [pltpu.with_memory_space_constraint(factor[0].T, pltpu.HBM) for factor in (left_in, right_in, basis)]
    copies = pl.pallas_call(
        copies_kernel,
        out_shape=shape((half, 2 * rank + 8, width), BF16),
        in_specs=[pl.BlockSpec(memory_space=pltpu.HBM)] * 3,
        out_specs=VMEM,
        scratch_shapes=[pltpu.VMEM((rank, tokens), BF16), pltpu.VMEM((8, width), F32), pltpu.SemaphoreType.DMA((3,))],
        compiler_params=limit(4),
    )(*own)
    mine = lax.all_to_all(copies, "dp", 0, 0, tiled=True, axis_index_groups=groups)
    theirs = lax.ppermute(mine, "dp", others)
    parity = (lax.axis_index("dp") & 1).astype(jnp.int32).reshape(1)
    x, left, rows, rebuilt, sums = pl.pallas_call(
        first_kernel,
        out_shape=(
            shape((tokens, features), BF16),
            shape((tokens, rank), BF16),
            shape((4, tokens, LANES), F32),
            shape((half, tokens, width), F32),
            shape((half, 8, width), F32),
        ),
        in_specs=[SMEM, pl.BlockSpec(memory_space=pltpu.HBM), VMEM, VMEM, VMEM],
        out_specs=(VMEM,) * 5,
        scratch_shapes=[pltpu.SemaphoreType.DMA((replicas,))],
        compiler_params=limit(20),
        cost_estimate=cost(24),
    )(parity, x_hbm, norm_gain, left_in[0].T, mine)
    power_t, kept, packed, send = pl.pallas_call(
        second_kernel,
        out_shape=(
            shape((rank, tokens), F32),
            shape((half, tokens, width), BF16),
            shape((8, width), F32),
            shape((half, height, width), BF16),
        ),
        in_specs=[SMEM] + [VMEM] * 7,
        out_specs=(VMEM,) * 4,
        scratch_shapes=[
            pltpu.VMEM((4, tokens, LANES), F32),
            pltpu.VMEM((half, tokens, width), F32),
            pltpu.VMEM((half, 8, width), F32),
            pltpu.VMEM((half, tokens, width), BF16),
            pltpu.VMEM((16, width), F32),
            pltpu.VMEM((24, LANES), F32),
        ],
        compiler_params=limit(32),
    )(parity, x, norm_gain, left, rows, rebuilt, mine, theirs)
    other = lax.ppermute(send, "dp", others)
    keep = pl.pallas_call(
        third_kernel,
        out_shape=shape((half, rank, width), F32),
        in_specs=[VMEM] * 2,
        out_specs=VMEM,
        compiler_params=limit(12),
        cost_estimate=cost(12),
    )(power_t, kept)
    payload = pl.pallas_call(
        pair_kernel,
        out_shape=shape((half, height, width), BF16),
        in_specs=[VMEM] * 4,
        out_specs=VMEM,
        scratch_shapes=[pltpu.VMEM((16, width), F32)],
        compiler_params=limit(12),
    )(keep, packed, sums, other)
    terms = lax.all_to_all(payload, "dp", 0, 0, tiled=True, axis_index_groups=groups)

    factor = float(1.0 / (tokens * replicas) ** 0.5)
    gain_sums, bias_sums, moved = pl.pallas_call(
        lambda *refs: post_kernel(factor, *refs),
        out_shape=(shape((1, width), F32), shape((1, width), F32), shape((rank, width + tokens), BF16)),
        in_specs=[VMEM, VMEM],
        out_specs=(VMEM,) * 3,
        scratch_shapes=[pltpu.VMEM((24, LANES), F32)],
        compiler_params=limit(16),
    )(terms, power_t)
    sections = lax.axis_size("section")
    moved = lax.ppermute(moved, "section", [(i, i - 1) for i in range(1, sections)])
    left_out, right_out, gain_grad, bias_grad = pl.pallas_call(
        place_kernel,
        out_shape=(shape((rank, tokens), BF16), shape((rank, width), BF16), shape((1, width), F32), shape((1, width), F32)),
        in_specs=[VMEM] * 3,
        out_specs=(pl.BlockSpec(memory_space=pltpu.HBM),) * 4,
        scratch_shapes=[pltpu.SemaphoreType.DMA((4,))],
        compiler_params=limit(4),
    )(moved, gain_sums, bias_sums)
    return gain_grad, bias_grad, left_out.T[None], right_out.T[None]


def solution(mesh):
    placed = (
        P("section", "dp", None),
        P("section", None),
        P("section", "dp", None),
        P("section", "dp", None),
        P("section", "dp", None),
    )
    return jax.shard_map(
        on_device,
        mesh=mesh,
        in_specs=placed,
        out_specs=(
            P("section", "dp"),
            P("section", "dp"),
            P("section", "dp", None),
            P("section", "dp", None),
        ),
        check_vma=False,
    )
```

```python
import jax
import jax.numpy as jnp
from jax import lax
from jax.experimental import pallas as pl
from jax.experimental.pallas import tpu as pltpu
from jax.sharding import PartitionSpec as P

LANES = 128
GROUP = 16
UNROLL = 8
FETCH = 2
F32 = jnp.float32
BF16 = jnp.bfloat16
NT = (((1,), (1,)), ((), ()))
EXACT = dict(precision=lax.Precision.HIGHEST, preferred_element_type=F32)
VMEM = pl.BlockSpec(memory_space=pltpu.VMEM)
SMEM = pl.BlockSpec(memory_space=pltpu.SMEM)


def fold(value):
    return value[:8] + value[8:]


def gain_pass(j, k, left, factors, x, gain, rows, rebuilt, sums, plain=True, normal=True):
    tokens, width = rebuilt.shape[1:]
    rank = left.shape[1]
    chunks = range(width // LANES)
    columns = [pl.ds(pl.multiple_of(j * width + c * LANES, LANES), LANES) for c in chunks]
    gains = [jnp.broadcast_to(gain[:, columns[c]], (GROUP, LANES)) for c in chunks]
    products = [jnp.zeros((8, LANES), F32) for _ in chunks]
    bare = [jnp.zeros((8, LANES), F32) for _ in chunks]
    if plain:
        rebuilt[k] = jnp.dot(left, factors[k, :rank, :], preferred_element_type=F32)
    for r in range(0, tokens, GROUP):
        group = slice(r, r + GROUP)
        if normal:
            mean, inverse, second = rows[0, group], rows[1, group], rows[3, group]
        if plain:
            first = rows[2, group]
        for c in chunks:
            part = rebuilt[k, group, c * LANES : (c + 1) * LANES]
            scaled = part * gains[c]
            if plain:
                first = first + scaled
                bare[c] = bare[c] + fold(part)
            if normal:
                normed = (x[group, columns[c]].astype(F32) - mean) * inverse
                second = second + scaled * normed
                products[c] = products[c] + fold(part * normed)
                rebuilt[k, group, c * LANES : (c + 1) * LANES] = scaled
        if plain:
            rows[2, group] = first
        if normal:
            rows[3, group] = second
    for c in chunks:
        lanes = slice(c * LANES, (c + 1) * LANES)
        if normal:
            sums[k, 0:1, lanes] = jnp.sum(products[c], axis=0, keepdims=True)
        if plain:
            sums[k, 1:2, lanes] = jnp.sum(bare[c], axis=0, keepdims=True)


def row_mean(total, features):
    return jnp.broadcast_to(jnp.sum(total, axis=1, keepdims=True) * (1.0 / features), total.shape)


def copies_kernel(left_t, right_t, basis_t, copies, left, packed, arrived):
    rank = left_t.shape[0]
    own = copies.at[0]
    fetches = [
        pltpu.make_async_copy(left_t, left, arrived.at[0]),
        pltpu.make_async_copy(right_t, own.at[:rank, :], arrived.at[1]),
        pltpu.make_async_copy(basis_t, own.at[rank : 2 * rank, :], arrived.at[2]),
    ]
    for fetch in fetches:
        fetch.start()
    fetches[0].wait()
    pack(lax.dot_general(left[...], left[...], NT, preferred_element_type=F32), packed)
    copies[0, 2 * rank :, :] = jnp.concatenate(split(packed[0:4, :], 2), axis=0).astype(BF16)
    for fetch in fetches[1:]:
        fetch.wait()
    for k in range(1, copies.shape[0]):
        copies[k] = copies[0]


def first_kernel(parity, x_hbm, gain, left_t, mine, x, left_out, rows, rebuilt, sums, arrived):
    half, _, width = mine.shape
    tokens, features = x.shape
    blocks = 2 * half
    chunks = range(width // LANES)

    def fetch(j):
        columns = pl.ds(pl.multiple_of(j * width, LANES), width)
        return pltpu.make_async_copy(x_hbm.at[:, columns], x.at[:, columns], arrived.at[j])

    @pl.loop(0, blocks)
    def _(j):
        fetch(j).start()

    left_out[...] = left_t[...].astype(F32).T.astype(BF16)
    left = left_out[...]
    rows[...] = jnp.zeros_like(rows)

    @pl.loop(0, half // UNROLL)
    def _(step):
        for k in [step * UNROLL + u for u in range(UNROLL)]:
            gain_pass(2 * k + parity[0], k, left, mine, x, gain, rows, rebuilt, sums, normal=False)

    for j in range(FETCH):
        fetch(j).wait()
    for r in range(0, tokens, GROUP):
        group = slice(r, r + GROUP)
        total = x[group, :LANES].astype(F32)
        for c in chunks[1:]:
            total = total + x[group, c * LANES : (c + 1) * LANES].astype(F32)
        rows[0, group] = row_mean(total, width)

    @pl.loop(0, blocks // FETCH)
    def _(step):
        @pl.when(step > 0)
        def _():
            for u in range(FETCH):
                fetch(step * FETCH + u).wait()

        for r in range(0, tokens, GROUP):
            group = slice(r, r + GROUP)
            base, total, squares = rows[0, group], rows[1, group], rows[3, group]
            for u in range(FETCH):
                for c in chunks:
                    start = (step * FETCH + u) * width + c * LANES
                    center = x[group, pl.ds(pl.multiple_of(start, LANES), LANES)].astype(F32) - base
                    total = total + center
                    squares = squares + center * center
            rows[1, group] = total
            rows[3, group] = squares

    shift = row_mean(rows[1], features)
    variance = jnp.maximum(row_mean(rows[3], features) - shift * shift, 0.0)
    rows[0] = rows[0] + shift
    rows[1] = lax.rsqrt(variance + 1e-05)
    rows[3] = jnp.zeros((tokens, LANES), F32)

    @pl.loop(0, half // UNROLL)
    def _(step):
        for k in [step * UNROLL + u for u in range(UNROLL)]:
            gain_pass(2 * k + parity[0], k, left, mine, x, gain, rows, rebuilt, sums, plain=False)


def second_kernel(
    parity, x, gain, left_ref, rows_in, rebuilt_mine, mine, theirs, power_t, kept, packed, send, rows, rebuilt, sums, moved, tail, square
):
    half, height, width = theirs.shape
    tokens, features = x.shape
    rank = left_ref.shape[1]
    chunks = range(width // LANES)
    left = left_ref[...]
    rows[...] = rows_in[...]

    ones = jnp.ones((GROUP, width), BF16)

    def mixing(k, totals):
        terms = []
        for side, factors in enumerate((mine, theirs)):
            start = (2 * k + (parity[0] ^ side)) * width
            terms.append(factors[k, :rank, :] * gain[:, pl.ds(pl.multiple_of(start, LANES), width)].astype(BF16))
        basis = jnp.concatenate([mine[k, rank : 2 * rank, :], theirs[k, rank : 2 * rank, :], ones], axis=0)
        both = lax.dot_general(basis, jnp.concatenate(terms + [ones], axis=0), NT, preferred_element_type=F32)
        near, far = slice(0, rank), slice(rank, 2 * rank)
        last = slice(2 * rank, 2 * rank + 1)
        spread = [factors[k, 2 * rank :, :].astype(F32) for factors in (mine, theirs)]
        values = (
            both[near, near] + both[far, far],
            both[near, last] + both[far, last],
            both[last, near] + both[last, far],
            spread[0] + spread[1],
        )
        return tuple(total + value for total, value in zip(totals, values))

    totals = (jnp.zeros((rank, rank), F32), jnp.zeros((rank, 1), F32), jnp.zeros((1, rank), F32), jnp.zeros((8, width), F32))
    for k in range(half):
        totals = mixing(k, totals)
        gain_pass(2 * k + (1 - parity[0]), k, left, theirs, x, gain, rows, rebuilt, sums)
    mixed = totals[0] - totals[1] * (totals[2] * (1.0 / features))
    spread = unpack(totals[3][0:4] + totals[3][4:8], square) * (1.0 / (2 * half * tokens))
    good = dict(precision=lax.Precision.HIGH, preferred_element_type=F32)
    near = lax.dot_general(jnp.dot(mixed, spread, **good), mixed, NT, **good)
    row = lax.broadcasted_iota(jnp.int32, near.shape, 0)
    col = lax.broadcasted_iota(jnp.int32, near.shape, 1)
    level = jnp.sum(jnp.where(row == col, near, 0.0)) * 1e-05 + 1e-08
    lines = []
    steps = eliminate(near + jnp.where(row == col, level, 0.0), lines, 0.25 * level)

    first = row_mean(rows[2], features)
    second = row_mean(rows[3], features)
    rows[2] = rows[1] * rows[1] * second
    rows[3] = rows[0] * rows[2] - rows[1] * first

    def project(side, factors, source, target):
        def step(k, total):
            j = 2 * k + (parity[0] ^ side)
            columns = [pl.ds(pl.multiple_of(j * width + c * LANES, LANES), LANES) for c in chunks]
            groups = []
            for r in range(0, tokens, GROUP):
                group = slice(r, r + GROUP)
                inverse, slope, offset = rows[1, group], rows[2, group], rows[3, group]
                values = []
                for c in chunks:
                    lanes = slice(c * LANES, (c + 1) * LANES)
                    value = source[k, group, lanes] * inverse - x[group, columns[c]].astype(F32) * slope + offset
                    values.append(value.astype(BF16))
                    target[k, group, lanes] = values[-1]
                groups.append(jnp.concatenate(values, axis=1))
            block = jnp.concatenate(groups, axis=0)
            return total + lax.dot_general(block, factors[k, rank : 2 * rank, :], NT, preferred_element_type=F32)

        return step

    power = jnp.zeros((tokens, rank), F32)
    for k in range(half):
        power = project(0, mine, rebuilt_mine, kept)(k, power)
        next(steps)
    for k in range(half):
        power = project(1, theirs, rebuilt, moved)(k, power)
    basis_change = jnp.concatenate(lines, axis=0)
    power = lax.dot_general(basis_change, power, NT, **EXACT)
    power_t[...] = power
    pack(lax.dot_general(power, power, NT, **EXACT), packed)
    high = power.astype(BF16)
    split_gram(packed[0:4, :], tail)

    @pl.loop(0, half // UNROLL)
    def _(step):
        for k in [step * UNROLL + u for u in range(UNROLL)]:
            terms = jnp.dot(high, moved[k], preferred_element_type=F32)
            send[k, :rank, :] = terms.astype(BF16)
            split_sums(sums[k, 0:2, :], tail)
            send[k, rank:, :] = tail[...].astype(BF16)


def split(value, count):
    terms = []
    for _ in range(count):
        terms.append(value.astype(BF16).astype(F32))
        value = value - terms[-1]
    return terms


def split_sums(value, tail):
    for i, term in enumerate(split(value, 2)):
        tail[2 * i : 2 * i + 2, :] = term


def split_gram(value, tail):
    for i, term in enumerate(split(value, 3)):
        tail[4 + 4 * i : 8 + 4 * i, :] = term


def pack(gram, packed):
    size = gram.shape[0]
    half, quarter = size // 2, size // 4
    per = packed.shape[1] // LANES
    corner = gram[half:, half:]
    upper = jnp.concatenate([gram[:quarter], gram[quarter:half]], axis=1)
    lower = jnp.concatenate([corner[8 * i : 8 * i + 8] for i in range(half // 8)], axis=1)
    packed[...] = jnp.zeros_like(packed)
    for q in range(quarter + 8):
        line = upper[q : q + 1] if q < quarter else lower[q - quarter : q - quarter + 1]
        packed[q // per : q // per + 1, (q % per) * LANES : (q % per + 1) * LANES] = line


def unpack(packed, square):
    lines = square.shape[0]
    per = packed.shape[1] // LANES
    quarter = lines - 8
    half = 2 * quarter
    for q in range(lines):
        square[q : q + 1, :] = packed[q // per : q // per + 1, (q % per) * LANES : (q % per + 1) * LANES]
    upper = jnp.concatenate([square[:quarter, : 2 * half], square[:quarter, 2 * half :]], axis=0)
    corner = jnp.concatenate([square[quarter:, half * i : half * (i + 1)] for i in range(half // 8)], axis=0)
    return jnp.concatenate([upper, jnp.concatenate([upper[:, half:].T, corner], axis=1)], axis=0)


def third_kernel(power_t, kept, keep):
    high = power_t[...].astype(BF16)

    @pl.loop(0, keep.shape[0] // UNROLL)
    def _(step):
        for k in [step * UNROLL + u for u in range(UNROLL)]:
            keep[k] = jnp.dot(high, kept[k], preferred_element_type=F32)


def pair_kernel(keep, packed, sums, other, out, tail):
    half, rank, _ = keep.shape
    theirs = other[0, rank:, :].astype(F32)
    split_gram(packed[0:4, :] + (theirs[4:8] + (theirs[8:12] + theirs[12:16])), tail)

    @pl.loop(0, half // UNROLL)
    def _(step):
        for k in [step * UNROLL + u for u in range(UNROLL)]:
            out[k, :rank, :] = (keep[k] + other[k, :rank, :].astype(F32)).astype(BF16)
            theirs = other[k, rank:, :].astype(F32)
            split_sums(sums[k, 0:2, :] + (theirs[0:2] + theirs[2:4]), tail)
            out[k, rank:, :] = tail[...].astype(BF16)


def eliminate(gram, done, floor=None):
    size = gram.shape[0]
    wide = 2 * size
    count = size // 8
    row = lax.broadcasted_iota(jnp.int32, (size, size), 0)
    col = lax.broadcasted_iota(jnp.int32, (size, size), 1)
    work = jnp.concatenate([gram, jnp.where(row == col, 1.0, 0.0).astype(F32)], axis=1)
    parts = [work[8 * i : 8 * i + 8] for i in range(count)]
    for b in range(count):
        below = range(b + 1, count)
        lines = [jnp.broadcast_to(parts[b][r : r + 1], (8, wide)) for r in range(8)]
        entry = {
            (i, j): jnp.broadcast_to(parts[b][i : i + 1, 8 * b + j : 8 * b + j + 1], (8, wide))
            for i in range(8)
            for j in range(i + 1)
        }
        factors = {(i, r): jnp.broadcast_to(parts[i][:, 8 * b + r : 8 * b + r + 1], (8, wide)) for i in below for r in range(8)}
        for r in range(8):
            if floor is not None:
                entry[r, r] = jnp.maximum(entry[r, r], floor)
            scale = 1.0 / entry[r, r]
            for i in below:
                factors[i, r] = factors[i, r] * scale
            for q in range(r + 1, 8):
                ratio = entry[q, r] * scale
                for j in range(r + 1, q + 1):
                    entry[q, j] = entry[q, j] - ratio * entry[j, r]
                for i in below:
                    factors[i, q] = factors[i, q] - factors[i, r] * entry[q, r]
                lines[q] = lines[q] - ratio * lines[r]
        done += [(lines[r] * lax.rsqrt(entry[r, r]))[:1, size:] for r in range(8)]
        for i in below:
            terms = [factors[i, r] * lines[r] for r in range(8)]
            while len(terms) > 1:
                terms = [terms[t] + terms[t + 1] for t in range(0, len(terms), 2)]
            parts[i] = parts[i] - terms[0]
        yield


def inverse_factor(gram):
    done = []
    for _ in eliminate(gram, done):
        pass
    return jnp.concatenate(done, axis=0)


def post_kernel(factor, terms, power_t, gain_out, bias_out, moved, square):
    rank, tokens = power_t.shape
    width = terms.shape[2]
    total = terms[0].astype(F32)
    for j in range(1, terms.shape[0]):
        total = total + terms[j].astype(F32)
    extra = total[rank:]
    gain_out[...] = (extra[0:1] + extra[2:3]) * factor
    bias_out[...] = (extra[1:2] + extra[3:4]) * factor
    inverse = inverse_factor(unpack(extra[4:8] + (extra[8:12] + extra[12:16]), square))
    moved[:, :width] = jnp.dot(inverse, total[:rank], **EXACT).astype(BF16)
    moved[:, width:] = jnp.dot(inverse, power_t[...], **EXACT).astype(BF16)


def place_kernel(moved, gain, bias, left_out, right_out, gain_out, bias_out, sent):
    width = right_out.shape[1]
    pairs = ((moved.at[:, :width], right_out), (moved.at[:, width:], left_out), (gain, gain_out), (bias, bias_out))
    copies = [pltpu.make_async_copy(source, target, sent.at[i]) for i, (source, target) in enumerate(pairs)]
    for copy in copies:
        copy.start()
    for copy in copies:
        copy.wait()


def limit(mib):
    return pltpu.CompilerParams(vmem_limit_bytes=mib * 2**20)


def cost(mib):
    return pl.CostEstimate(flops=0, bytes_accessed=mib * 2**20, transcendentals=0)


def on_device(saved_input, norm_gain, left_in, right_in, basis):
    _, tokens, features = saved_input.shape
    width, rank = right_in.shape[1:]
    replicas = lax.axis_size("dp")
    half = replicas // 2
    height = rank + 16
    others = [(i, i ^ 1) for i in range(replicas)]
    groups = [[2 * k + c for k in range(half)] for c in range(2)]
    shape = jax.ShapeDtypeStruct

    x_hbm = pltpu.with_memory_space_constraint(saved_input[0], pltpu.HBM)
    own = [pltpu.with_memory_space_constraint(factor[0].T, pltpu.HBM) for factor in (left_in, right_in, basis)]
    copies = pl.pallas_call(
        copies_kernel,
        out_shape=shape((half, 2 * rank + 8, width), BF16),
        in_specs=[pl.BlockSpec(memory_space=pltpu.HBM)] * 3,
        out_specs=VMEM,
        scratch_shapes=[pltpu.VMEM((rank, tokens), BF16), pltpu.VMEM((8, width), F32), pltpu.SemaphoreType.DMA((3,))],
        compiler_params=limit(4),
    )(*own)
    mine = lax.all_to_all(copies, "dp", 0, 0, tiled=True, axis_index_groups=groups)
    theirs = lax.ppermute(mine, "dp", others)
    parity = (lax.axis_index("dp") & 1).astype(jnp.int32).reshape(1)
    x, left, rows, rebuilt, sums = pl.pallas_call(
        first_kernel,
        out_shape=(
            shape((tokens, features), BF16),
            shape((tokens, rank), BF16),
            shape((4, tokens, LANES), F32),
            shape((half, tokens, width), F32),
            shape((half, 8, width), F32),
        ),
        in_specs=[SMEM, pl.BlockSpec(memory_space=pltpu.HBM), VMEM, VMEM, VMEM],
        out_specs=(VMEM,) * 5,
        scratch_shapes=[pltpu.SemaphoreType.DMA((replicas,))],
        compiler_params=limit(20),
        cost_estimate=cost(24),
    )(parity, x_hbm, norm_gain, left_in[0].T, mine)
    power_t, kept, packed, send = pl.pallas_call(
        second_kernel,
        out_shape=(
            shape((rank, tokens), F32),
            shape((half, tokens, width), BF16),
            shape((8, width), F32),
            shape((half, height, width), BF16),
        ),
        in_specs=[SMEM] + [VMEM] * 7,
        out_specs=(VMEM,) * 4,
        scratch_shapes=[
            pltpu.VMEM((4, tokens, LANES), F32),
            pltpu.VMEM((half, tokens, width), F32),
            pltpu.VMEM((half, 8, width), F32),
            pltpu.VMEM((half, tokens, width), BF16),
            pltpu.VMEM((16, width), F32),
            pltpu.VMEM((24, LANES), F32),
        ],
        compiler_params=limit(32),
    )(parity, x, norm_gain, left, rows, rebuilt, mine, theirs)
    other = lax.ppermute(send, "dp", others)
    keep = pl.pallas_call(
        third_kernel,
        out_shape=shape((half, rank, width), F32),
        in_specs=[VMEM] * 2,
        out_specs=VMEM,
        compiler_params=limit(12),
        cost_estimate=cost(12),
    )(power_t, kept)
    payload = pl.pallas_call(
        pair_kernel,
        out_shape=shape((half, height, width), BF16),
        in_specs=[VMEM] * 4,
        out_specs=VMEM,
        scratch_shapes=[pltpu.VMEM((16, width), F32)],
        compiler_params=limit(12),
    )(keep, packed, sums, other)
    terms = lax.all_to_all(payload, "dp", 0, 0, tiled=True, axis_index_groups=groups)

    factor = float(1.0 / (tokens * replicas) ** 0.5)
    gain_sums, bias_sums, moved = pl.pallas_call(
        lambda *refs: post_kernel(factor, *refs),
        out_shape=(shape((1, width), F32), shape((1, width), F32), shape((rank, width + tokens), BF16)),
        in_specs=[VMEM, VMEM],
        out_specs=(VMEM,) * 3,
        scratch_shapes=[pltpu.VMEM((24, LANES), F32)],
        compiler_params=limit(16),
    )(terms, power_t)
    sections = lax.axis_size("section")
    moved = lax.ppermute(moved, "section", [(i, i - 1) for i in range(1, sections)])
    left_out, right_out, gain_grad, bias_grad = pl.pallas_call(
        place_kernel,
        out_shape=(shape((rank, tokens), BF16), shape((rank, width), BF16), shape((1, width), F32), shape((1, width), F32)),
        in_specs=[VMEM] * 3,
        out_specs=(pl.BlockSpec(memory_space=pltpu.HBM),) * 4,
        scratch_shapes=[pltpu.SemaphoreType.DMA((4,))],
        compiler_params=limit(4),
    )(moved, gain_sums, bias_sums)
    return gain_grad, bias_grad, left_out.T[None], right_out.T[None]


def solution(mesh):
    placed = (
        P("section", "dp", None),
        P("section", None),
        P("section", "dp", None),
        P("section", "dp", None),
        P("section", "dp", None),
    )
    return jax.shard_map(
        on_device,
        mesh=mesh,
        in_specs=placed,
        out_specs=(
            P("section", "dp"),
            P("section", "dp"),
            P("section", "dp", None),
            P("section", "dp", None),
        ),
        check_vma=False,
    )
```
